32 devices in a mesh: seq: 8 (over z, x), head: 4 (over y, core).
Axes of the slice: x: 2, y: 2, z: 4, core: 2. Of those that a mesh axis runs over, the one named last changes fastest.
Arguments:
- xs: bfloat16 [12288, 1280], P('seq', 'head'), may hold values from -6 to 6
- dxs: bfloat16 [12288, 1280], P('seq', 'head'), may hold values from -6 to 6
- zgate: bfloat16 [12288, 1280], P('seq', 'head'), may hold values from -6 to 6
- bmat: bfloat16 [12288, 128], P('seq'), may hold values from -1 to 1
- cmat: bfloat16 [12288, 128], P('seq'), may hold values from -1 to 1
- dt_raw: float32 [20, 12288], P('head', 'seq'), may hold values from -3 to 3
- dt_bias: float32 [20], P('head'), may hold values from -1 to 1
- a_rate: float32 [20], P('head'), may hold values from 0 to 1, as said below
- d_skip: float32 [20], P('head'), may hold values from 0.5 to 2
- gain: float32 [1280], replicated, may hold values from 0.5 to 1.5
- traj_ids: int32 [48], P('seq'), may hold values from 0 to 3, as said below
Outputs:
- normed: bfloat16 [12288, 1280], P(('seq', 'head'))
- normed_tan: bfloat16 [12288, 1280], P(('seq', 'head'))
The draws below stay inside these ranges and needn't reach their ends.
Inputs may be any that keep to these rules, and one draw needn't show every extreme that they name: `traj_ids`: never falling from one block to the next; trajectory 0 spans exactly the first 24 blocks, trajectory 1 the next 6 blocks or more, every other trajectory one block or more. `a_rate`: positive.
All inputs are finite; a program needn't handle non-finite values.
Results may differ from the reference program's by a relative error of at most 0.0057.
Values may be sent and summed in bfloat16 or wider, within the bound.
A program may use at most 128 MiB of HBM per device.

```python
import jax
import jax.numpy as jnp
from jax import lax

P_SIZE = 64
N = 128
Q = 256
BLK_DEV = 6
HEADS = 20
INNER = 1280
TOKENS = 12288
NBLOCKS = 48
TRAJS = 4


def draw_a_rate(key, part):
    pick_key, spread_key = jax.random.split(key)
    slow_share = 0.5
    slow_flag = jax.random.uniform(pick_key, (HEADS,), jnp.float32) < slow_share
    position = jax.random.uniform(spread_key, (HEADS,), jnp.float32)
    slow_low = jnp.log(jnp.float32(0.2 / TOKENS))
    slow_high = jnp.log(jnp.float32(2.0 / TOKENS))
    boundary = jnp.log(jnp.float32(60.0 / TOKENS))
    slow_rate = jnp.exp(slow_low + (slow_high - slow_low) * position)
    fast_rate = jnp.exp(boundary * (1.0 - position))
    return jnp.where(slow_flag, slow_rate, fast_rate).astype(jnp.float32)


def draw_traj_ids(key, part):
    first_span = NBLOCKS // 2
    rest_blocks = NBLOCKS - first_span
    cut_count = TRAJS - 2
    pool = rest_blocks - BLK_DEV
    cuts = jax.random.permutation(jax.random.fold_in(key, 7), jnp.arange(pool, dtype=jnp.int32))[:cut_count] + BLK_DEV
    marks = jnp.zeros((rest_blocks,), jnp.int32).at[cuts].set(1)
    rest_ids = jnp.cumsum(marks).astype(jnp.int32) + 1
    return jnp.concatenate([jnp.zeros((first_span,), jnp.int32), rest_ids]).astype(jnp.int32)


def level_of(stream_key, extent, pieces, least, top_value):
    loudness = 1.0
    for axis_at, parts in pieces:
        steps = jax.random.uniform(jax.random.fold_in(jax.random.fold_in(stream_key, 6), axis_at), (parts,), jnp.float32, least / len(pieces), top_value / len(pieces))
        loudness = loudness * jnp.repeat(jnp.exp(steps), extent[axis_at] // parts).reshape((-1,) + (1,) * (len(extent) - 1 - axis_at))
    return loudness


def gaussian(key, shape, spread, reach, cuts=(), kind=jnp.bfloat16):
    entries = jax.random.normal(key, shape, jnp.float32) * spread
    if len(cuts) > 0:
        entries = level_of(key, shape, cuts, -0.22, 0.18) * entries
    return jnp.clip(entries, min=-reach, max=reach).astype(kind)


def setup_inputs(seed: int = 0) -> dict:
    streams_of = jax.random.split(jax.random.key(seed), 12)
    xs = gaussian(streams_of[0], (TOKENS, INNER), 1.0, 6.0, ((0, 8), (1, 4)))
    dxs = gaussian(streams_of[1], (TOKENS, INNER), 1.0, 6.0, ((0, 8), (1, 4)))
    zgate = gaussian(streams_of[2], (TOKENS, INNER), 1.0, 6.0, ((0, 8), (1, 4)))
    bmat = gaussian(streams_of[3], (TOKENS, N), 0.15, 1.0, ((0, 8),))
    cmat = gaussian(streams_of[4], (TOKENS, N), 0.15, 1.0, ((0, 8),))
    dt_raw = gaussian(streams_of[5], (HEADS, TOKENS), 0.5, 3.0, ((0, 4), (1, 8)), jnp.float32)
    dt_bias = jnp.clip(jax.random.uniform(streams_of[6], (HEADS,), jnp.float32, -1.0, 1.0) * level_of(streams_of[6], (HEADS,), ((0, 4),), -0.4, 0.0), -1.0, 1.0)
    a_rate = draw_a_rate(jax.random.fold_in(streams_of[11], 71), 0)
    d_skip = jnp.clip(0.5 + 1.5 * jax.random.uniform(streams_of[8], (HEADS,), jnp.float32) ** level_of(streams_of[8], (HEADS,), ((0, 4),), -0.2, 0.2), 0.5, 2.0)
    gain = jnp.clip(1.0 + 0.1 * jax.random.normal(streams_of[9], (INNER,), jnp.float32), 0.5, 1.5)
    traj_ids = draw_traj_ids(jax.random.fold_in(streams_of[11], 71), 0)
    return {"xs": xs, "dxs": dxs, "zgate": zgate, "bmat": bmat, "cmat": cmat, "dt_raw": dt_raw, "dt_bias": dt_bias, "a_rate": a_rate, "d_skip": d_skip, "gain": gain, "traj_ids": traj_ids}


def block_terms(joined, b_block, c_block, step_block, log_block, state_in):
    token_count = joined.shape[0]
    scores = jnp.dot(c_block, b_block.T, preferred_element_type=jnp.float32)
    places = jnp.arange(token_count)
    causal_mask = places[:, None] >= places[None, :]
    log_gap = log_block[:, :, None] - log_block[:, None, :]
    decay_table = jnp.exp(jnp.where(causal_mask[None], log_gap, -jnp.inf))
    weights = (scores[None] * decay_table * step_block[:, None, :]).astype(jnp.bfloat16)
    y_diag = jnp.einsum('hts,shp->thp', weights.astype(jnp.float32), joined.astype(jnp.float32))
    end_log = log_block[:, -1]
    weight_in = step_block * jnp.exp(end_log[:, None] - log_block)
    weighted = (joined.astype(jnp.float32) * weight_in.T[:, :, None]).astype(jnp.bfloat16)
    block_state = jnp.einsum('shp,sn->hpn', weighted.astype(jnp.float32), b_block.astype(jnp.float32))
    y_off = jnp.einsum('tn,hpn->thp', c_block.astype(jnp.float32), state_in, precision=lax.Precision.HIGHEST) * jnp.exp(log_block).T[:, :, None]
    leaving = jnp.exp(end_log)[:, None, None] * state_in + block_state
    return (y_diag + y_off, leaving)

def reference(xs, dxs, zgate, bmat, cmat, dt_raw, dt_bias, a_rate, d_skip, gain, traj_ids):
    step_size = jax.nn.softplus(dt_raw + dt_bias[:, None])
    step_blocks = step_size.reshape(HEADS, NBLOCKS, Q).transpose(1, 0, 2)
    log_blocks = jnp.cumsum(-(step_blocks * a_rate[None, :, None]), axis=-1)
    joined = jnp.concatenate([xs.reshape(NBLOCKS, Q, HEADS, P_SIZE), dxs.reshape(NBLOCKS, Q, HEADS, P_SIZE)], axis=-1)
    keep_flags = jnp.concatenate([jnp.zeros((1,), jnp.float32), (traj_ids[1:] == traj_ids[:-1]).astype(jnp.float32)])

    def advance(carried, item):
        joined_block, b_block, c_block, step_block, log_block, keep_flag = item
        state_in = keep_flag * carried
        y_block, leaving = block_terms(joined_block, b_block, c_block, step_block, log_block, state_in)
        return (leaving, y_block)
    zero_state = jnp.zeros((HEADS, 2 * P_SIZE, N), jnp.float32)
    items = (joined, bmat.reshape(NBLOCKS, Q, N), cmat.reshape(NBLOCKS, Q, N), step_blocks, log_blocks, keep_flags)
    _, y_blocks = lax.scan(advance, zero_state, items)
    y_total = y_blocks + joined.astype(jnp.float32) * d_skip[None, None, :, None]
    y_joined = y_total.reshape(TOKENS, HEADS, 2 * P_SIZE).astype(jnp.bfloat16)
    y_main = y_joined[:, :, :P_SIZE].reshape(TOKENS, INNER)
    y_tan = y_joined[:, :, P_SIZE:].reshape(TOKENS, INNER)
    gate_value = jax.nn.silu(zgate.astype(jnp.float32))
    gated = y_main.astype(jnp.float32) * gate_value
    gated_tan = y_tan.astype(jnp.float32) * gate_value
    mean_square = lax.optimization_barrier(jnp.mean(gated * gated, axis=-1, keepdims=True))
    mean_cross = lax.optimization_barrier(jnp.mean(gated * gated_tan, axis=-1, keepdims=True))
    inv_rms = lax.rsqrt(mean_square + 1e-05)
    normed = (gain * gated * inv_rms).astype(jnp.bfloat16)
    normed_tan = (gain * (gated_tan * inv_rms - gated * inv_rms ** 3 * mean_cross)).astype(jnp.bfloat16)
    return (normed, normed_tan)
```

```python
import functools

import jax
import jax.numpy as jnp
from jax import lax
from jax.experimental import pallas as pl
from jax.experimental.pallas import tpu as pltpu
from jax.sharding import PartitionSpec as P

Q = 256
HALF = 128
TAIL = 16
MESH = pl.DeviceIdType.MESH
F32 = jnp.float32
BF16 = jnp.bfloat16


def column_of(ref, count):
    place = lax.broadcasted_iota(jnp.int32, (8, 1), 0)
    column = jnp.zeros((8, 1), F32)
    for h in range(count):
        column = jnp.where(place == h, ref[h], column)
    return column


def kernel(
    n_seq, n_head, heads, blocks, rows,
    xs, dxs, zg, bm, cm, dt, bias, rate, skip, gain, traj,
    out_main, out_tan,
    dt8, joined, bt, bstate, lrow, wrow, lcol, dec, part, scale, smsg, sgot, enter, gsend, got,
    s_send, s_recv, g_send, g_recv, own_sem,
):
    chain = n_seq // 2
    seq = lax.axis_index("seq")
    me = lax.axis_index("head")
    rank = lax.rem(seq, chain)
    base = seq - rank

    barrier = pltpu.get_barrier_semaphore()
    for o in range(1, n_head):
        pl.semaphore_signal(
            barrier, inc=1, device_id=(seq, lax.rem(me + o, n_head)), device_id_type=MESH
        )
    for o in range(1, chain):
        pl.semaphore_signal(
            barrier, inc=1, device_id=(base + lax.rem(rank + o, chain), me), device_id_type=MESH
        )

    dt8[...] = jnp.zeros(dt8.shape, F32)
    dt8[0:heads, :] = dt[...]
    step_all = jax.nn.softplus(dt8[...] + column_of(bias, heads))
    fall_all = step_all * column_of(rate, heads)
    step = jnp.concatenate([step_all[:, c * Q:(c + 1) * Q] for c in range(blocks)], axis=0)
    fall = jnp.concatenate([fall_all[:, c * Q:(c + 1) * Q] for c in range(blocks)], axis=0)
    first = fall.astype(BF16)
    rest = fall - first.astype(F32)
    second = rest.astype(BF16)
    third = (rest - second.astype(F32)).astype(BF16)
    upper = (
        lax.broadcasted_iota(jnp.int32, (Q, Q), 0) <= lax.broadcasted_iota(jnp.int32, (Q, Q), 1)
    ).astype(F32).astype(BF16)
    sums = [jnp.dot(x, upper, preferred_element_type=F32) for x in (first, second, third)]
    log_decay = -(sums[0] + (sums[1] + sums[2]))
    end_log = log_decay[:, Q - 1:Q]
    weight_in = step * jnp.exp(end_log - log_decay)
    log_row = log_decay - jnp.log(step)
    end_wide = jnp.broadcast_to(end_log, (blocks * 8, 128))
    end_decay = jnp.exp(end_wide)
    whole_log = end_wide[0:8]
    for c in range(1, blocks):
        whole_log = whole_log + end_wide[c * 8:(c + 1) * 8]
    factor = jnp.exp(whole_log)
    turned = jnp.concatenate([log_decay, jnp.zeros((128 - blocks * 8, Q), F32)], axis=0).T
    for c in range(blocks):
        lrow[c] = log_row[c * 8:(c + 1) * 8]
        wrow[c] = weight_in[c * 8:(c + 1) * 8]
        dec[c] = end_decay[c * 8:(c + 1) * 8]
        lcol[c] = turned[:, c * 8:(c + 1) * 8]
        bt[c] = bm[c * Q:(c + 1) * Q, :].astype(F32).T

    def keep_after(c):
        return jnp.where(traj[c] == traj[c + 1], 1.0, 0.0).astype(F32)

    def s_copy(h, d, to):
        return pltpu.make_async_remote_copy(
            src_ref=smsg.at[h],
            dst_ref=sgot.at[d - 1, h],
            send_sem=s_send.at[d - 1, h],
            recv_sem=s_recv.at[d - 1, h],
            device_id=(to, me),
            device_id_type=MESH,
        )

    last_id = traj[blocks - 1].astype(F32)
    tail_row = lax.broadcasted_iota(jnp.int32, (TAIL, 128), 0)
    for h in range(heads):
        low = h * 64
        joined[h] = jnp.concatenate([xs[:, low:low + 64], dxs[:, low:low + 64]], axis=1)
        state = None
        for c in range(blocks):
            weighted = (bt[c] * wrow[c, h:h + 1, :]).astype(BF16)
            block = jnp.dot(
                weighted, joined[h, c * Q:(c + 1) * Q, :], preferred_element_type=F32
            )
            bstate[h, c] = block
            if c == 0:
                state = block
            else:
                state = keep_after(c - 1) * (dec[c, h:h + 1, :] * state) + block
        smsg[h, 0:128, :] = state.astype(BF16)
        whole = jnp.broadcast_to(factor[h:h + 1, :], (TAIL, 128))
        high = whole.astype(BF16).astype(F32)
        tail = jnp.where(tail_row == 0, high, jnp.where(tail_row == 1, whole - high, last_id))
        smsg[h, 128:128 + TAIL, :] = tail.astype(BF16)
        if h == 0:
            pl.semaphore_wait(barrier, (n_head - 1) + (chain - 1))
        for d in range(chain - 1, 0, -1):
            @pl.when(rank + d < chain)
            def _():
                s_copy(h, d, seq + d).start()

    row_at = lax.broadcasted_iota(jnp.int32, (HALF, HALF), 0)
    col_at = lax.broadcasted_iota(jnp.int32, (HALF, HALF), 1)
    causal = row_at >= col_at

    def inner(c, carry):
        at = pl.ds(pl.multiple_of(c * Q, Q), Q)
        scores = lax.dot_general(
            cm[at, :], bm[at, :], (((1,), (1,)), ((), ())), preferred_element_type=F32
        )
        top = jnp.where(causal, scores[0:HALF, 0:HALF], 0.0)
        left = scores[HALF:Q, 0:HALF]
        corner = jnp.where(causal, scores[HALF:Q, HALF:Q], 0.0)
        for h in range(heads):
            low = h * 64
            row = lrow[c, h:h + 1, :]
            wide = jnp.broadcast_to(lcol[c, :, h:h + 1], (Q, HALF))
            gate_in = zg[at, low:low + 64].astype(F32)
            gate_half = gate_in / (1.0 + jnp.exp(-gate_in))
            gate = jnp.concatenate([gate_half, gate_half], axis=1)
            w_top = top * jnp.exp(jnp.minimum(wide[0:HALF] - row[:, 0:HALF], 4.0))
            w_left = left * jnp.exp(wide[HALF:Q] - row[:, 0:HALF])
            w_corner = corner * jnp.exp(jnp.minimum(wide[HALF:Q] - row[:, HALF:Q], 4.0))
            values = joined[h, at, :]
            y_top = jnp.dot(w_top.astype(BF16), values[0:HALF], preferred_element_type=F32)
            y_low = jnp.dot(
                jnp.concatenate([w_left.astype(BF16), w_corner.astype(BF16)], axis=1),
                values,
                preferred_element_type=F32,
            )
            y = jnp.concatenate([y_top, y_low], axis=0) + skip[h] * values.astype(F32)
            part[h, at, :] = y * gate
            scale[h, at, :] = jnp.exp(wide) * gate
        return carry

    lax.fori_loop(0, blocks, inner, 0)

    def g_copy(h, o):
        to = lax.rem(me + o, n_head)
        return pltpu.make_async_remote_copy(
            src_ref=gsend.at[h, pl.ds(pl.multiple_of(to * rows, 16), rows), :],
            dst_ref=got.at[me, h],
            send_sem=g_send.at[o - 1, h],
            recv_sem=g_recv.at[o - 1, h],
            device_id=(seq, to),
            device_id_type=MESH,
        )

    def own_copy(h):
        return pltpu.make_async_copy(
            gsend.at[h, pl.ds(pl.multiple_of(me * rows, 16), rows), :], got.at[me, h], own_sem.at[h]
        )

    order = sorted(range(1, n_head), key=lambda o: abs(o - n_head // 2))
    first_id = traj[0].astype(F32)
    for h in range(heads):
        enter[...] = jnp.zeros(enter.shape, F32)
        for d in range(chain - 1, 0, -1):
            @pl.when(rank >= d)
            def _():
                s_copy(h, d, seq - d).wait_recv()
                tail = sgot[d - 1, h, 128:128 + TAIL, :].astype(F32)
                passed = tail[0:1] + tail[1:2]
                same = jnp.where(tail[2:3] == first_id, 1.0, 0.0)
                enter[...] = passed * enter[...] + same * sgot[d - 1, h, 0:128, :].astype(F32)
        state = enter[...]
        for c in range(blocks):
            at = slice(c * Q, (c + 1) * Q)
            carried = jnp.dot(cm[at, :], state.astype(BF16), preferred_element_type=F32)
            gsend[h, at, :] = (part[h, at, :] + carried * scale[h, at, :]).astype(BF16)
            if c < blocks - 1:
                state = keep_after(c) * (dec[c, h:h + 1, :] * state + bstate[h, c])
        for o in order:
            g_copy(h, o).start()
        own_copy(h).start()

    for h in range(heads):
        own_copy(h).wait()
        for o in order:
            g_copy(h, o).wait_recv()

    pairs = n_head * heads // 2
    width = n_head * heads * 64
    span = 32
    left_lanes = lax.broadcasted_iota(jnp.int32, (span, 128), 1) < 64

    def norm(i, carry):
        at = pl.ds(pl.multiple_of(i * span, span), span)
        square = jnp.zeros((span, 128), F32)
        cross = jnp.zeros((span, 128), F32)
        for j in range(pairs):
            k, m = 2 * j, 2 * j + 1
            one = got[k // heads, k % heads, at, :].astype(F32)
            two = got[m // heads, m % heads, at, :].astype(F32)
            main = jnp.where(left_lanes, one, pltpu.roll(two, 64, 1))
            tan = jnp.where(left_lanes, pltpu.roll(one, 64, 1), two)
            square += main * main
            cross += main * tan
            out_main[at, j * 128:(j + 1) * 128] = main.astype(BF16)
            out_tan[at, j * 128:(j + 1) * 128] = tan.astype(BF16)
        mean_square = jnp.sum(square, axis=1, keepdims=True) / width
        mean_cross = jnp.sum(cross, axis=1, keepdims=True) / width
        inv = lax.rsqrt(mean_square + 1e-05)
        inv_wide = jnp.broadcast_to(inv, (span, 128))
        pull = jnp.broadcast_to(inv * inv * inv * mean_cross, (span, 128))
        for j in range(pairs):
            lanes = slice(j * 128, (j + 1) * 128)
            by = gain[lanes].reshape(1, 128)
            main = out_main[at, lanes].astype(F32)
            tan = out_tan[at, lanes].astype(F32)
            out_main[at, lanes] = (by * main * inv_wide).astype(BF16)
            out_tan[at, lanes] = (by * (tan * inv_wide - main * pull)).astype(BF16)
        return carry

    lax.fori_loop(0, rows // span, norm, 0)

    for h in range(heads):
        for o in order:
            g_copy(h, o).wait_send()
        for d in range(chain - 1, 0, -1):
            @pl.when(rank + d < chain)
            def _():
                s_copy(h, d, seq + d).wait_send()


def local(n_seq, n_head, xs, dxs, zgate, bmat, cmat, dt_raw, dt_bias, a_rate, d_skip, gain, traj_ids):
    tokens = xs.shape[0]
    heads = dt_raw.shape[0]
    blocks = tokens // Q
    rows = tokens // n_head
    width = xs.shape[1] * n_head
    chain = n_seq // 2
    vmem = pl.BlockSpec(memory_space=pltpu.VMEM)
    smem = pl.BlockSpec(memory_space=pltpu.SMEM)
    return pl.pallas_call(
        functools.partial(kernel, n_seq, n_head, heads, blocks, rows),
        out_shape=[jax.ShapeDtypeStruct((rows, width), BF16)] * 2,
        in_specs=[vmem] * 6 + [smem] * 3 + [vmem, smem],
        out_specs=[vmem] * 2,
        scratch_shapes=[
            pltpu.VMEM((8, tokens), F32),
            pltpu.VMEM((heads, tokens, 128), BF16),
            pltpu.VMEM((blocks, 128, Q), F32),
            pltpu.VMEM((heads, blocks, 128, 128), F32),
            pltpu.VMEM((blocks, 8, Q), F32),
            pltpu.VMEM((blocks, 8, Q), F32),
            pltpu.VMEM((blocks, Q, 8), F32),
            pltpu.VMEM((blocks, 8, 128), F32),
            pltpu.VMEM((heads, tokens, 128), F32),
            pltpu.VMEM((heads, tokens, 128), F32),
            pltpu.VMEM((heads, 128 + TAIL, 128), BF16),
            pltpu.VMEM((chain - 1, heads, 128 + TAIL, 128), BF16),
            pltpu.VMEM((128, 128), F32),
            pltpu.VMEM((heads, tokens, 128), BF16),
            pltpu.VMEM((n_head, heads, rows, 128), BF16),
            pltpu.SemaphoreType.DMA((chain - 1, heads)),
            pltpu.SemaphoreType.DMA((chain - 1, heads)),
            pltpu.SemaphoreType.DMA((n_head - 1, heads)),
            pltpu.SemaphoreType.DMA((n_head - 1, heads)),
            pltpu.SemaphoreType.DMA((heads,)),
        ],
        compiler_params=pltpu.CompilerParams(
            collective_id=0, has_side_effects=True, vmem_limit_bytes=56 * 2**20
        ),
        name="ssd_layer",
    )(xs, dxs, zgate, bmat, cmat, dt_raw, dt_bias, a_rate, d_skip, gain, traj_ids)


def solution(mesh):
    placed = (
        P("seq", "head"), P("seq", "head"), P("seq", "head"), P("seq", None), P("seq", None),
        P("head", "seq"), P("head"), P("head"), P("head"), P(), P("seq"),
    )
    return jax.shard_map(
        functools.partial(local, mesh.shape["seq"], mesh.shape["head"]),
        mesh=mesh,
        in_specs=placed,
        out_specs=(P(("seq", "head"), None), P(("seq", "head"), None)),
        check_vma=False,
    )
```

```python
import functools

import jax
import jax.numpy as jnp
from jax import lax
from jax.experimental import pallas as pl
from jax.experimental.pallas import tpu as pltpu
from jax.sharding import PartitionSpec as P

Q = 256
HALF = 128
TAIL = 16
MESH = pl.DeviceIdType.MESH
F32 = jnp.float32
BF16 = jnp.bfloat16


def column_of(ref, count):
    place = lax.broadcasted_iota(jnp.int32, (8, 1), 0)
    column = jnp.zeros((8, 1), F32)
    for h in range(count):
        column = jnp.where(place == h, ref[h], column)
    return column


def by_rows(one, two):
    return lax.dot_general(one, two, (((1,), (1,)), ((), ())), preferred_element_type=F32)


def kernel(
    n_seq, n_head, heads, blocks, rows,
    xs, dxs, zg, bm, cm, dt, bias, rate, skip, gain, traj,
    out_main, out_tan,
    dt8, bstate, lrow, wrow, erow, lcol, dec, table, part, scale, smsg, sgot, enter, gsend, got,
    s_send, s_recv, g_send, g_recv, own_sem,
):
    chain = n_seq // 2
    seq = lax.axis_index("seq")
    me = lax.axis_index("head")
    rank = lax.rem(seq, chain)
    base = seq - rank

    barrier = pltpu.get_barrier_semaphore()
    for o in range(1, n_head):
        pl.semaphore_signal(
            barrier, inc=1, device_id=(seq, lax.rem(me + o, n_head)), device_id_type=MESH
        )
    for o in range(1, chain):
        pl.semaphore_signal(
            barrier, inc=1, device_id=(base + lax.rem(rank + o, chain), me), device_id_type=MESH
        )

    dt8[...] = jnp.zeros(dt8.shape, F32)
    dt8[0:heads, :] = dt[...]
    step_all = jax.nn.softplus(dt8[...] + column_of(bias, heads))
    fall_all = step_all * column_of(rate, heads)
    step = jnp.concatenate([step_all[:, c * Q:(c + 1) * Q] for c in range(blocks)], axis=0)
    fall = jnp.concatenate([fall_all[:, c * Q:(c + 1) * Q] for c in range(blocks)], axis=0)
    first = fall.astype(BF16)
    rest = fall - first.astype(F32)
    second = rest.astype(BF16)
    third = (rest - second.astype(F32)).astype(BF16)
    upper = (
        lax.broadcasted_iota(jnp.int32, (Q, Q), 0) <= lax.broadcasted_iota(jnp.int32, (Q, Q), 1)
    ).astype(F32).astype(BF16)
    sums = [jnp.dot(x, upper, preferred_element_type=F32) for x in (first, second, third)]
    log_decay = -(sums[0] + (sums[1] + sums[2]))
    end_log = log_decay[:, Q - 1:Q]
    weight_in = step * jnp.exp(end_log - log_decay)
    end_wide = jnp.broadcast_to(end_log, (blocks * 8, 128))
    end_decay = jnp.exp(end_wide)
    whole_log = end_wide[0:8]
    for c in range(1, blocks):
        whole_log = whole_log + end_wide[c * 8:(c + 1) * 8]
    factor = jnp.exp(whole_log)
    for c in range(blocks):
        wrow[c] = weight_in[c * 8:(c + 1) * 8]
        dec[c] = end_decay[c * 8:(c + 1) * 8]

    def keep_after(c):
        return jnp.where(traj[c] == traj[c + 1], 1.0, 0.0).astype(F32)

    def values_of(h, c):
        low, at = h * 64, slice(c * Q, (c + 1) * Q)
        return jnp.concatenate([xs[low:low + 64, at], dxs[low:low + 64, at]], axis=0)

    def s_copy(h, d, to):
        return pltpu.make_async_remote_copy(
            src_ref=smsg.at[h],
            dst_ref=sgot.at[d - 1, h],
            send_sem=s_send.at[d - 1, h],
            recv_sem=s_recv.at[d - 1, h],
            device_id=(to, me),
            device_id_type=MESH,
        )

    last_id = traj[blocks - 1].astype(F32)
    tail_row = lax.broadcasted_iota(jnp.int32, (TAIL, 128), 0)
    for h in range(heads):
        state = None
        for c in range(blocks):
            weighted = (values_of(h, c).astype(F32) * wrow[c, h:h + 1, :]).astype(BF16)
            block = jnp.dot(weighted, bm[c * Q:(c + 1) * Q, :], preferred_element_type=F32)
            bstate[h, c] = block
            if c == 0:
                state = block
            else:
                state = keep_after(c - 1) * (dec[c, h:h + 1, :] * state) + block
        smsg[h, 0:128, :] = state.astype(BF16)
        whole = jnp.broadcast_to(factor[h:h + 1, :], (TAIL, 128))
        high = whole.astype(BF16).astype(F32)
        tail = jnp.where(tail_row == 0, high, jnp.where(tail_row == 1, whole - high, last_id))
        smsg[h, 128:128 + TAIL, :] = tail.astype(BF16)
        if h == 0:
            pl.semaphore_wait(barrier, (n_head - 1) + (chain - 1))
        for d in range(chain - 1, 0, -1):
            @pl.when(rank + d < chain)
            def _():
                s_copy(h, d, seq + d).start()

    log_row = log_decay - jnp.log(step)
    decay = jnp.exp(log_decay)
    turned = jnp.concatenate([log_decay, jnp.zeros((128 - blocks * 8, Q), F32)], axis=0).T
    row_at = lax.broadcasted_iota(jnp.int32, (Q, Q), 0)
    col_at = lax.broadcasted_iota(jnp.int32, (Q, Q), 1)
    causal = row_at >= col_at
    for c in range(blocks):
        lrow[c] = log_row[c * 8:(c + 1) * 8]
        erow[c] = decay[c * 8:(c + 1) * 8]
        lcol[c] = turned[:, c * 8:(c + 1) * 8]
        at = slice(c * Q, (c + 1) * Q)
        table[c] = jnp.where(causal, by_rows(cm[at, :], bm[at, :]), 0.0)

    def g_copy(h, o):
        to = lax.rem(me + o, n_head)
        return pltpu.make_async_remote_copy(
            src_ref=gsend.at[h, pl.ds(pl.multiple_of(to * rows, 16), rows), :],
            dst_ref=got.at[me, h],
            send_sem=g_send.at[o - 1, h],
            recv_sem=g_recv.at[o - 1, h],
            device_id=(seq, to),
            device_id_type=MESH,
        )

    def own_copy(h):
        return pltpu.make_async_copy(
            gsend.at[h, pl.ds(pl.multiple_of(me * rows, 16), rows), :], got.at[me, h], own_sem.at[h]
        )

    order = sorted(range(1, n_head), key=lambda o: abs(o - n_head // 2))
    first_id = traj[0].astype(F32)
    for h in range(heads):
        low = h * 64
        for c in range(blocks):
            at = slice(c * Q, (c + 1) * Q)
            row = lrow[c, h:h + 1, :]
            wide = jnp.broadcast_to(lcol[c, :, h:h + 1], (Q, HALF))
            gate_in = zg[low:low + 64, at].astype(F32)
            gate = gate_in / (1.0 + jnp.exp(-gate_in))
            w_top = table[c, 0:HALF, 0:HALF] * jnp.exp(
                jnp.minimum(wide[0:HALF] - row[:, 0:HALF], 4.0)
            )
            w_left = table[c, HALF:Q, 0:HALF] * jnp.exp(wide[HALF:Q] - row[:, 0:HALF])
            w_corner = table[c, HALF:Q, HALF:Q] * jnp.exp(
                jnp.minimum(wide[HALF:Q] - row[:, HALF:Q], 4.0)
            )
            w_low = jnp.concatenate([w_left.astype(BF16), w_corner.astype(BF16)], axis=1)
            values = values_of(h, c)
            y = jnp.concatenate(
                [by_rows(values[:, 0:HALF], w_top.astype(BF16)), by_rows(values, w_low)], axis=1
            )
            y = y + skip[h] * values.astype(F32)
            part[c] = y * jnp.concatenate([gate, gate], axis=0)
            scale[c] = erow[c, h:h + 1, :] * gate

        enter[...] = jnp.zeros(enter.shape, F32)
        for d in range(chain - 1, 0, -1):
            @pl.when(rank >= d)
            def _():
                s_copy(h, d, seq - d).wait_recv()
                tail = sgot[d - 1, h, 128:128 + TAIL, :].astype(F32)
                passed = tail[0:1] + tail[1:2]
                same = jnp.where(tail[2:3] == first_id, 1.0, 0.0)
                enter[...] = passed * enter[...] + same * sgot[d - 1, h, 0:128, :].astype(F32)
        state = enter[...]
        for c in range(blocks):
            at = slice(c * Q, (c + 1) * Q)
            carried = by_rows(state.astype(BF16), cm[at, :])
            scaled = scale[c]
            gated = part[c] + carried * jnp.concatenate([scaled, scaled], axis=0)
            gsend[h, at, :] = gated.T.astype(BF16)
            if c < blocks - 1:
                state = keep_after(c) * (dec[c, h:h + 1, :] * state + bstate[h, c])
        for o in order:
            g_copy(h, o).start()
        own_copy(h).start()

    for h in range(heads):
        own_copy(h).wait()
        for o in order:
            g_copy(h, o).wait_recv()

    pairs = n_head * heads // 2
    width = n_head * heads * 64
    span = 32
    left_lanes = lax.broadcasted_iota(jnp.int32, (span, 128), 1) < 64

    def norm(i, carry):
        at = pl.ds(pl.multiple_of(i * span, span), span)
        square = jnp.zeros((span, 128), F32)
        cross = jnp.zeros((span, 128), F32)
        for j in range(pairs):
            k, m = 2 * j, 2 * j + 1
            one = got[k // heads, k % heads, at, :].astype(F32)
            two = got[m // heads, m % heads, at, :].astype(F32)
            main = jnp.where(left_lanes, one, pltpu.roll(two, 64, 1))
            tan = jnp.where(left_lanes, pltpu.roll(one, 64, 1), two)
            square += main * main
            cross += main * tan
            out_main[at, j * 128:(j + 1) * 128] = main.astype(BF16)
            out_tan[at, j * 128:(j + 1) * 128] = tan.astype(BF16)
        mean_square = jnp.sum(square, axis=1, keepdims=True) / width
        mean_cross = jnp.sum(cross, axis=1, keepdims=True) / width
        inv = lax.rsqrt(mean_square + 1e-05)
        inv_wide = jnp.broadcast_to(inv, (span, 128))
        pull = jnp.broadcast_to(inv * inv * inv * mean_cross, (span, 128))
        for j in range(pairs):
            lanes = slice(j * 128, (j + 1) * 128)
            by = gain[lanes].reshape(1, 128)
            main = out_main[at, lanes].astype(F32)
            tan = out_tan[at, lanes].astype(F32)
            out_main[at, lanes] = (by * main * inv_wide).astype(BF16)
            out_tan[at, lanes] = (by * (tan * inv_wide - main * pull)).astype(BF16)
        return carry

    lax.fori_loop(0, rows // span, norm, 0)

    for h in range(heads):
        for o in order:
            g_copy(h, o).wait_send()
        for d in range(chain - 1, 0, -1):
            @pl.when(rank + d < chain)
            def _():
                s_copy(h, d, seq + d).wait_send()


def local(n_seq, n_head, xs, dxs, zgate, bmat, cmat, dt_raw, dt_bias, a_rate, d_skip, gain, traj_ids):
    tokens = xs.shape[0]
    heads = dt_raw.shape[0]
    blocks = tokens // Q
    rows = tokens // n_head
    width = xs.shape[1] * n_head
    chain = n_seq // 2
    vmem = pl.BlockSpec(memory_space=pltpu.VMEM)
    smem = pl.BlockSpec(memory_space=pltpu.SMEM)
    return pl.pallas_call(
        functools.partial(kernel, n_seq, n_head, heads, blocks, rows),
        out_shape=[jax.ShapeDtypeStruct((rows, width), BF16)] * 2,
        in_specs=[vmem] * 6 + [smem] * 3 + [vmem, smem],
        out_specs=[vmem] * 2,
        scratch_shapes=[
            pltpu.VMEM((8, tokens), F32),
            pltpu.VMEM((heads, blocks, 128, 128), F32),
            pltpu.VMEM((blocks, 8, Q), F32),
            pltpu.VMEM((blocks, 8, Q), F32),
            pltpu.VMEM((blocks, 8, Q), F32),
            pltpu.VMEM((blocks, Q, 8), F32),
            pltpu.VMEM((blocks, 8, 128), F32),
            pltpu.VMEM((blocks, Q, Q), F32),
            pltpu.VMEM((blocks, 128, Q), F32),
            pltpu.VMEM((blocks, 64, Q), F32),
            pltpu.VMEM((heads, 128 + TAIL, 128), BF16),
            pltpu.VMEM((chain - 1, heads, 128 + TAIL, 128), BF16),
            pltpu.VMEM((128, 128), F32),
            pltpu.VMEM((heads, tokens, 128), BF16),
            pltpu.VMEM((n_head, heads, rows, 128), BF16),
            pltpu.SemaphoreType.DMA((chain - 1, heads)),
            pltpu.SemaphoreType.DMA((chain - 1, heads)),
            pltpu.SemaphoreType.DMA((n_head - 1, heads)),
            pltpu.SemaphoreType.DMA((n_head - 1, heads)),
            pltpu.SemaphoreType.DMA((heads,)),
        ],
        compiler_params=pltpu.CompilerParams(
            collective_id=0, has_side_effects=True, vmem_limit_bytes=32 * 2**20
        ),
        name="ssd_layer",
    )(xs.T, dxs.T, zgate.T, bmat, cmat, dt_raw, dt_bias, a_rate, d_skip, gain, traj_ids)


def solution(mesh):
    placed = (
        P("seq", "head"), P("seq", "head"), P("seq", "head"), P("seq", None), P("seq", None),
        P("head", "seq"), P("head"), P("head"), P("head"), P(), P("seq"),
    )
    return jax.shard_map(
        functools.partial(local, mesh.shape["seq"], mesh.shape["head"]),
        mesh=mesh,
        in_specs=placed,
        out_specs=(P(("seq", "head"), None), P(("seq", "head"), None)),
        check_vma=False,
    )
```

```python
import functools

import jax
import jax.numpy as jnp
from jax import lax
from jax.experimental import pallas as pl
from jax.experimental.pallas import tpu as pltpu
from jax.sharding import PartitionSpec as P

Q = 256
HALF = 128
TAIL = 16
MESH = pl.DeviceIdType.MESH
F32 = jnp.float32
BF16 = jnp.bfloat16


def column_of(ref, count):
    place = lax.broadcasted_iota(jnp.int32, (8, 1), 0)
    column = jnp.zeros((8, 1), F32)
    for h in range(count):
        column = jnp.where(place == h, ref[h], column)
    return column


def by_rows(one, two):
    return lax.dot_general(one, two, (((1,), (1,)), ((), ())), preferred_element_type=F32)


def kernel(
    n_seq, n_head, heads, blocks, rows,
    xs_hbm, dxs_hbm, zg_hbm, bm_hbm, cm_hbm, dt_hbm, bias_hbm, rate_hbm, skip_hbm, gain_hbm, traj_hbm,
    out_main, out_tan,
    xs, dxs, zg, bm, cm, dt, bias, rate, skip, gain, traj, in_sem,
    dt8, bstate, lrow, wrow, erow, lcol, dec, table, part, scale, smsg, sgot, enter, gsend, got,
    s_send, s_recv, g_send, g_recv, own_sem,
):
    chain = n_seq // 2
    seq = lax.axis_index("seq")
    me = lax.axis_index("head")
    rank = lax.rem(seq, chain)
    base = seq - rank

    fetches = [
        pltpu.make_async_copy(source, target, in_sem.at[i])
        for i, (source, target) in enumerate((
            (dt_hbm, dt), (bias_hbm, bias), (rate_hbm, rate), (xs_hbm, xs), (dxs_hbm, dxs),
            (bm_hbm, bm), (traj_hbm, traj), (cm_hbm, cm), (zg_hbm, zg), (skip_hbm, skip),
            (gain_hbm, gain),
        ))
    ]
    for fetch in fetches:
        fetch.start()

    barrier = pltpu.get_barrier_semaphore()
    for o in range(1, n_head):
        pl.semaphore_signal(
            barrier, inc=1, device_id=(seq, lax.rem(me + o, n_head)), device_id_type=MESH
        )
    for o in range(1, chain):
        pl.semaphore_signal(
            barrier, inc=1, device_id=(base + lax.rem(rank + o, chain), me), device_id_type=MESH
        )

    dt8[...] = jnp.zeros(dt8.shape, F32)
    for fetch in fetches[0:3]:
        fetch.wait()
    dt8[0:heads, :] = dt[...]
    step_all = jax.nn.softplus(dt8[...] + column_of(bias, heads))
    fall_all = step_all * column_of(rate, heads)
    step = jnp.concatenate([step_all[:, c * Q:(c + 1) * Q] for c in range(blocks)], axis=0)
    fall = jnp.concatenate([fall_all[:, c * Q:(c + 1) * Q] for c in range(blocks)], axis=0)
    first = fall.astype(BF16)
    rest = fall - first.astype(F32)
    second = rest.astype(BF16)
    third = (rest - second.astype(F32)).astype(BF16)
    upper = (
        lax.broadcasted_iota(jnp.int32, (Q, Q), 0) <= lax.broadcasted_iota(jnp.int32, (Q, Q), 1)
    ).astype(F32).astype(BF16)
    sums = [jnp.dot(x, upper, preferred_element_type=F32) for x in (first, second, third)]
    log_decay = -(sums[0] + (sums[1] + sums[2]))
    end_log = log_decay[:, Q - 1:Q]
    weight_in = step * jnp.exp(end_log - log_decay)
    end_wide = jnp.broadcast_to(end_log, (blocks * 8, 128))
    end_decay = jnp.exp(end_wide)
    whole_log = end_wide[0:8]
    for c in range(1, blocks):
        whole_log = whole_log + end_wide[c * 8:(c + 1) * 8]
    factor = jnp.exp(whole_log)
    for c in range(blocks):
        wrow[c] = weight_in[c * 8:(c + 1) * 8]
        dec[c] = end_decay[c * 8:(c + 1) * 8]

    def keep_after(c):
        return jnp.where(traj[c] == traj[c + 1], 1.0, 0.0).astype(F32)

    def values_of(h, c):
        low, at = h * 64, slice(c * Q, (c + 1) * Q)
        return jnp.concatenate([xs[low:low + 64, at], dxs[low:low + 64, at]], axis=0)

    def s_copy(h, d, to):
        return pltpu.make_async_remote_copy(
            src_ref=smsg.at[h],
            dst_ref=sgot.at[d - 1, h],
            send_sem=s_send.at[d - 1, h],
            recv_sem=s_recv.at[d - 1, h],
            device_id=(to, me),
            device_id_type=MESH,
        )

    for fetch in fetches[3:7]:
        fetch.wait()
    last_id = traj[blocks - 1].astype(F32)
    tail_row = lax.broadcasted_iota(jnp.int32, (TAIL, 128), 0)
    for h in range(heads):
        state = None
        for c in range(blocks):
            weighted = (values_of(h, c).astype(F32) * wrow[c, h:h + 1, :]).astype(BF16)
            block = jnp.dot(weighted, bm[c * Q:(c + 1) * Q, :], preferred_element_type=F32)
            bstate[h, c] = block
            if c == 0:
                state = block
            else:
                state = keep_after(c - 1) * (dec[c, h:h + 1, :] * state) + block
        smsg[h, 0:128, :] = state.astype(BF16)
        whole = jnp.broadcast_to(factor[h:h + 1, :], (TAIL, 128))
        high = whole.astype(BF16).astype(F32)
        tail = jnp.where(tail_row == 0, high, jnp.where(tail_row == 1, whole - high, last_id))
        smsg[h, 128:128 + TAIL, :] = tail.astype(BF16)
        if h == 0:
            pl.semaphore_wait(barrier, (n_head - 1) + (chain - 1))
        for d in range(chain - 1, 0, -1):
            @pl.when(rank + d < chain)
            def _():
                s_copy(h, d, seq + d).start()

    for fetch in fetches[7:]:
        fetch.wait()
    log_row = log_decay - jnp.log(step)
    decay = jnp.exp(log_decay)
    turned = jnp.concatenate([log_decay, jnp.zeros((128 - blocks * 8, Q), F32)], axis=0).T
    row_at = lax.broadcasted_iota(jnp.int32, (Q, Q), 0)
    col_at = lax.broadcasted_iota(jnp.int32, (Q, Q), 1)
    causal = row_at >= col_at
    for c in range(blocks):
        lrow[c] = log_row[c * 8:(c + 1) * 8]
        erow[c] = decay[c * 8:(c + 1) * 8]
        lcol[c] = turned[:, c * 8:(c + 1) * 8]
        at = slice(c * Q, (c + 1) * Q)
        table[c] = jnp.where(causal, by_rows(cm[at, :], bm[at, :]), 0.0)

    def g_copy(h, o, i):
        to = lax.rem(me + o, n_head)
        return pltpu.make_async_remote_copy(
            src_ref=gsend.at[h, pl.ds(pl.multiple_of(to * rows + i * span, 16), span), :],
            dst_ref=got.at[me, h, pl.ds(i * span, span), :],
            send_sem=g_send.at[o - 1, h, i],
            recv_sem=g_recv.at[o - 1, h, i],
            device_id=(seq, to),
            device_id_type=MESH,
        )

    def own_copy(h):
        return pltpu.make_async_copy(
            gsend.at[h, pl.ds(pl.multiple_of(me * rows, 16), rows), :], got.at[me, h], own_sem.at[h]
        )

    span = 128 if rows % 128 == 0 else rows
    pieces = rows // span
    order = sorted(range(1, n_head), key=lambda o: abs(o - n_head // 2))
    first_id = traj[0].astype(F32)
    for h in range(heads):
        low = h * 64
        for c in range(blocks):
            at = slice(c * Q, (c + 1) * Q)
            row = lrow[c, h:h + 1, :]
            wide = jnp.broadcast_to(lcol[c, :, h:h + 1], (Q, HALF))
            gate_in = zg[low:low + 64, at].astype(F32)
            gate = gate_in / (1.0 + jnp.exp(-gate_in))
            w_top = table[c, 0:HALF, 0:HALF] * jnp.exp(
                jnp.minimum(wide[0:HALF] - row[:, 0:HALF], 4.0)
            )
            w_left = table[c, HALF:Q, 0:HALF] * jnp.exp(wide[HALF:Q] - row[:, 0:HALF])
            w_corner = table[c, HALF:Q, HALF:Q] * jnp.exp(
                jnp.minimum(wide[HALF:Q] - row[:, HALF:Q], 4.0)
            )
            w_low = jnp.concatenate([w_left.astype(BF16), w_corner.astype(BF16)], axis=1)
            values = values_of(h, c)
            y = jnp.concatenate(
                [by_rows(values[:, 0:HALF], w_top.astype(BF16)), by_rows(values, w_low)], axis=1
            )
            y = y + skip[h] * values.astype(F32)
            part[c] = y * jnp.concatenate([gate, gate], axis=0)
            scale[c] = erow[c, h:h + 1, :] * gate

        enter[...] = jnp.zeros(enter.shape, F32)
        for d in range(chain - 1, 0, -1):
            @pl.when(rank >= d)
            def _():
                s_copy(h, d, seq - d).wait_recv()
                tail = sgot[d - 1, h, 128:128 + TAIL, :].astype(F32)
                passed = tail[0:1] + tail[1:2]
                same = jnp.where(tail[2:3] == first_id, 1.0, 0.0)
                enter[...] = passed * enter[...] + same * sgot[d - 1, h, 0:128, :].astype(F32)
        state = enter[...]
        for c in range(blocks):
            at = slice(c * Q, (c + 1) * Q)
            carried = by_rows(state.astype(BF16), cm[at, :])
            scaled = scale[c]
            gated = part[c] + carried * jnp.concatenate([scaled, scaled], axis=0)
            gsend[h, at, :] = gated.T.astype(BF16)
            if c < blocks - 1:
                state = keep_after(c) * (dec[c, h:h + 1, :] * state + bstate[h, c])
        own_copy(h).start()
        if h < heads - 2:
            for o in order:
                for i in range(pieces):
                    g_copy(h, o, i).start()
    for i in range(pieces):
        for h in range(heads - 2, heads):
            for o in order:
                g_copy(h, o, i).start()

    for h in range(heads):
        own_copy(h).wait()

    pairs = n_head * heads // 2
    width = n_head * heads * 64
    step_rows = 32
    left_lanes = lax.broadcasted_iota(jnp.int32, (step_rows, 128), 1) < 64

    def norm(i, carry):
        at = pl.ds(pl.multiple_of(i * step_rows, step_rows), step_rows)
        square = jnp.zeros((step_rows, 128), F32)
        cross = jnp.zeros((step_rows, 128), F32)
        for j in range(pairs):
            k, m = 2 * j, 2 * j + 1
            one = got[k // heads, k % heads, at, :].astype(F32)
            two = got[m // heads, m % heads, at, :].astype(F32)
            main = jnp.where(left_lanes, one, pltpu.roll(two, 64, 1))
            tan = jnp.where(left_lanes, pltpu.roll(one, 64, 1), two)
            square += main * main
            cross += main * tan
            out_main[at, j * 128:(j + 1) * 128] = main.astype(BF16)
            out_tan[at, j * 128:(j + 1) * 128] = tan.astype(BF16)
        mean_square = jnp.sum(square, axis=1, keepdims=True) / width
        mean_cross = jnp.sum(cross, axis=1, keepdims=True) / width
        inv = lax.rsqrt(mean_square + 1e-05)
        inv_wide = jnp.broadcast_to(inv, (step_rows, 128))
        pull = jnp.broadcast_to(inv * inv * inv * mean_cross, (step_rows, 128))
        for j in range(pairs):
            lanes = slice(j * 128, (j + 1) * 128)
            by = gain[lanes].reshape(1, 128)
            main = out_main[at, lanes].astype(F32)
            tan = out_tan[at, lanes].astype(F32)
            out_main[at, lanes] = (by * main * inv_wide).astype(BF16)
            out_tan[at, lanes] = (by * (tan * inv_wide - main * pull)).astype(BF16)
        return carry

    for i in range(pieces):
        for h in range(heads):
            for o in order:
                g_copy(h, o, i).wait_recv()
        steps = span // step_rows
        lax.fori_loop(i * steps, (i + 1) * steps, norm, 0)

    for h in range(heads):
        for o in order:
            for i in range(pieces):
                g_copy(h, o, i).wait_send()
        for d in range(chain - 1, 0, -1):
            @pl.when(rank + d < chain)
            def _():
                s_copy(h, d, seq + d).wait_send()


def local(n_seq, n_head, xs, dxs, zgate, bmat, cmat, dt_raw, dt_bias, a_rate, d_skip, gain, traj_ids):
    tokens = xs.shape[0]
    heads = dt_raw.shape[0]
    blocks = tokens // Q
    rows = tokens // n_head
    width = xs.shape[1] * n_head
    chain = n_seq // 2
    vmem = pl.BlockSpec(memory_space=pltpu.VMEM)
    hbm = pl.BlockSpec(memory_space=pltpu.HBM)
    span = 128 if rows % 128 == 0 else rows
    return pl.pallas_call(
        functools.partial(kernel, n_seq, n_head, heads, blocks, rows),
        out_shape=[jax.ShapeDtypeStruct((rows, width), BF16)] * 2,
        in_specs=[hbm] * 11,
        out_specs=[vmem] * 2,
        scratch_shapes=[
            pltpu.VMEM((xs.shape[1], tokens), BF16),
            pltpu.VMEM((xs.shape[1], tokens), BF16),
            pltpu.VMEM((xs.shape[1], tokens), BF16),
            pltpu.VMEM(bmat.shape, BF16),
            pltpu.VMEM(cmat.shape, BF16),
            pltpu.VMEM(dt_raw.shape, F32),
            pltpu.SMEM(dt_bias.shape, F32),
            pltpu.SMEM(a_rate.shape, F32),
            pltpu.SMEM(d_skip.shape, F32),
            pltpu.VMEM(gain.shape, F32),
            pltpu.SMEM(traj_ids.shape, jnp.int32),
            pltpu.SemaphoreType.DMA((11,)),
            pltpu.VMEM((8, tokens), F32),
            pltpu.VMEM((heads, blocks, 128, 128), F32),
            pltpu.VMEM((blocks, 8, Q), F32),
            pltpu.VMEM((blocks, 8, Q), F32),
            pltpu.VMEM((blocks, 8, Q), F32),
            pltpu.VMEM((blocks, Q, 8), F32),
            pltpu.VMEM((blocks, 8, 128), F32),
            pltpu.VMEM((blocks, Q, Q), F32),
            pltpu.VMEM((blocks, 128, Q), F32),
            pltpu.VMEM((blocks, 64, Q), F32),
            pltpu.VMEM((heads, 128 + TAIL, 128), BF16),
            pltpu.VMEM((chain - 1, heads, 128 + TAIL, 128), BF16),
            pltpu.VMEM((128, 128), F32),
            pltpu.VMEM((heads, tokens, 128), BF16),
            pltpu.VMEM((n_head, heads, rows, 128), BF16),
            pltpu.SemaphoreType.DMA((chain - 1, heads)),
            pltpu.SemaphoreType.DMA((chain - 1, heads)),
            pltpu.SemaphoreType.DMA((n_head - 1, heads, rows // span)),
            pltpu.SemaphoreType.DMA((n_head - 1, heads, rows // span)),
            pltpu.SemaphoreType.DMA((heads,)),
        ],
        compiler_params=pltpu.CompilerParams(
            collective_id=0, has_side_effects=True, vmem_limit_bytes=56 * 2**20
        ),
        name="ssd_layer",
    )(xs.T, dxs.T, zgate.T, bmat, cmat, dt_raw, dt_bias, a_rate, d_skip, gain, traj_ids)


def solution(mesh):
    placed = (
        P("seq", "head"), P("seq", "head"), P("seq", "head"), P("seq", None), P("seq", None),
        P("head", "seq"), P("head"), P("head"), P("head"), P(), P("seq"),
    )
    return jax.shard_map(
        functools.partial(local, mesh.shape["seq"], mesh.shape["head"]),
        mesh=mesh,
        in_specs=placed,
        out_specs=(P(("seq", "head"), None), P(("seq", "head"), None)),
        check_vma=False,
    )
```

```python
import functools

import jax
import jax.numpy as jnp
from jax import lax
from jax.experimental import pallas as pl
from jax.experimental.pallas import tpu as pltpu
from jax.sharding import PartitionSpec as P

Q = 256
HALF = 128
TAIL = 16
MESH = pl.DeviceIdType.MESH
F32 = jnp.float32
BF16 = jnp.bfloat16


def column_of(ref, count):
    place = lax.broadcasted_iota(jnp.int32, (8, 1), 0)
    column = jnp.zeros((8, 1), F32)
    for h in range(count):
        column = jnp.where(place == h, ref[h], column)
    return column


def by_rows(one, two):
    return lax.dot_general(one, two, (((1,), (1,)), ((), ())), preferred_element_type=F32)


def kernel(
    n_seq, n_head, heads, blocks, rows,
    xs_hbm, dxs_hbm, zg_hbm, bm_hbm, cm_hbm, dt_hbm, bias_hbm, rate_hbm, skip_hbm, gain_hbm, traj_hbm,
    out_main, out_tan,
    xs, dxs, zg, bm, cm, dt, bias, rate, skip, gain, traj, in_sem,
    dt8, bstate, lrow, wrow, erow, lcol, dec, table, cmt, part, scale, smsg, sgot, enter, gsend, got,
    s_send, s_recv, g_send, g_recv, own_sem,
):
    chain = n_seq // 2
    seq = lax.axis_index("seq")
    me = lax.axis_index("head")
    rank = lax.rem(seq, chain)
    base = seq - rank

    fetches = [
        pltpu.make_async_copy(source, target, in_sem.at[i])
        for i, (source, target) in enumerate((
            (dt_hbm, dt), (bias_hbm, bias), (rate_hbm, rate),
            (xs_hbm.at[0:64], xs.at[0:64]), (dxs_hbm.at[0:64], dxs.at[0:64]),
            (bm_hbm, bm), (traj_hbm, traj),
            (xs_hbm.at[64:], xs.at[64:]), (dxs_hbm.at[64:], dxs.at[64:]),
            (cm_hbm, cm), (zg_hbm, zg), (skip_hbm, skip), (gain_hbm, gain),
        ))
    ]
    for fetch in fetches:
        fetch.start()

    barrier = pltpu.get_barrier_semaphore()
    for o in range(1, n_head):
        pl.semaphore_signal(
            barrier, inc=1, device_id=(seq, lax.rem(me + o, n_head)), device_id_type=MESH
        )
    for o in range(1, chain):
        pl.semaphore_signal(
            barrier, inc=1, device_id=(base + lax.rem(rank + o, chain), me), device_id_type=MESH
        )

    dt8[...] = jnp.zeros(dt8.shape, F32)
    for fetch in fetches[0:3]:
        fetch.wait()
    dt8[0:heads, :] = dt[...]
    step_all = jax.nn.softplus(dt8[...] + column_of(bias, heads))
    fall_all = step_all * column_of(rate, heads)
    step = jnp.concatenate([step_all[:, c * Q:(c + 1) * Q] for c in range(blocks)], axis=0)
    fall = jnp.concatenate([fall_all[:, c * Q:(c + 1) * Q] for c in range(blocks)], axis=0)
    first = fall.astype(BF16)
    rest = fall - first.astype(F32)
    second = rest.astype(BF16)
    third = (rest - second.astype(F32)).astype(BF16)
    upper = (
        lax.broadcasted_iota(jnp.int32, (Q, Q), 0) <= lax.broadcasted_iota(jnp.int32, (Q, Q), 1)
    ).astype(F32).astype(BF16)
    sums = [jnp.dot(x, upper, preferred_element_type=F32) for x in (first, second, third)]
    log_decay = -(sums[0] + (sums[1] + sums[2]))
    end_log = log_decay[:, Q - 1:Q]
    weight_in = step * jnp.exp(end_log - log_decay)
    end_wide = jnp.broadcast_to(end_log, (blocks * 8, 128))
    end_decay = jnp.exp(end_wide)
    whole_log = end_wide[0:8]
    for c in range(1, blocks):
        whole_log = whole_log + end_wide[c * 8:(c + 1) * 8]
    factor = jnp.exp(whole_log)
    for c in range(blocks):
        wrow[c] = weight_in[c * 8:(c + 1) * 8]
        dec[c] = end_decay[c * 8:(c + 1) * 8]

    def keep_after(c):
        return jnp.where(traj[c] == traj[c + 1], 1.0, 0.0).astype(F32)

    def values_of(h, c):
        low, at = h * 64, slice(c * Q, (c + 1) * Q)
        return jnp.concatenate([xs[low:low + 64, at], dxs[low:low + 64, at]], axis=0)

    def s_copy(h, d, to):
        return pltpu.make_async_remote_copy(
            src_ref=smsg.at[h],
            dst_ref=sgot.at[d - 1, h],
            send_sem=s_send.at[d - 1, h],
            recv_sem=s_recv.at[d - 1, h],
            device_id=(to, me),
            device_id_type=MESH,
        )

    for fetch in fetches[3:7]:
        fetch.wait()
    last_id = traj[blocks - 1].astype(F32)
    tail_row = lax.broadcasted_iota(jnp.int32, (TAIL, 128), 0)
    for h in range(heads):
        if h == 1:
            for fetch in fetches[7:9]:
                fetch.wait()
        state = None
        for c in range(blocks):
            weighted = (values_of(h, c).astype(F32) * wrow[c, h:h + 1, :]).astype(BF16)
            block = jnp.dot(weighted, bm[c * Q:(c + 1) * Q, :], preferred_element_type=F32)
            bstate[h, c] = block
            if c == 0:
                state = block
            else:
                state = keep_after(c - 1) * (dec[c, h:h + 1, :] * state) + block
        smsg[h, 0:128, :] = state.astype(BF16)
        whole = jnp.broadcast_to(factor[h:h + 1, :], (TAIL, 128))
        high = whole.astype(BF16).astype(F32)
        tail = jnp.where(tail_row == 0, high, jnp.where(tail_row == 1, whole - high, last_id))
        smsg[h, 128:128 + TAIL, :] = tail.astype(BF16)
        if h == 0:
            pl.semaphore_wait(barrier, (n_head - 1) + (chain - 1))
        for d in range(chain - 1, 0, -1):
            @pl.when(rank + d < chain)
            def _():
                s_copy(h, d, seq + d).start()

    for fetch in fetches[9:]:
        fetch.wait()
    log_row = log_decay - jnp.log(step)
    decay = jnp.exp(log_decay)
    turned = jnp.concatenate([log_row, jnp.zeros((128 - blocks * 8, Q), F32)], axis=0).T
    row_at = lax.broadcasted_iota(jnp.int32, (Q, Q), 0)
    col_at = lax.broadcasted_iota(jnp.int32, (Q, Q), 1)
    causal = row_at <= col_at
    for c in range(blocks):
        lrow[c] = log_decay[c * 8:(c + 1) * 8]
        erow[c] = decay[c * 8:(c + 1) * 8]
        lcol[c] = turned[:, c * 8:(c + 1) * 8]
        at = slice(c * Q, (c + 1) * Q)
        table[c] = jnp.where(causal, by_rows(bm[at, :], cm[at, :]), 0.0)
        cmt[c] = cm[at, :].astype(F32).T.astype(BF16)

    def g_copy(h, o, i):
        to = lax.rem(me + o, n_head)
        return pltpu.make_async_remote_copy(
            src_ref=gsend.at[h, pl.ds(pl.multiple_of(to * rows + i * span, 16), span), :],
            dst_ref=got.at[me, h, pl.ds(i * span, span), :],
            send_sem=g_send.at[o - 1, h, i],
            recv_sem=g_recv.at[o - 1, h, i],
            device_id=(seq, to),
            device_id_type=MESH,
        )

    def own_copy(h):
        return pltpu.make_async_copy(
            gsend.at[h, pl.ds(pl.multiple_of(me * rows, 16), rows), :], got.at[me, h], own_sem.at[h]
        )

    span = 128 if rows % 128 == 0 else rows
    pieces = rows // span
    order = sorted(range(1, n_head), key=lambda o: abs(o - n_head // 2))
    first_id = traj[0].astype(F32)
    for h in range(heads):
        low = h * 64
        for c in range(blocks):
            at = slice(c * Q, (c + 1) * Q)
            row = lrow[c, h:h + 1, :]
            wide = jnp.broadcast_to(lcol[c, :, h:h + 1], (Q, HALF))
            gate_in = zg[low:low + 64, at].astype(F32)
            gate = gate_in / (1.0 + jnp.exp(-gate_in))
            w_top = table[c, 0:HALF, 0:HALF] * jnp.exp(
                jnp.minimum(row[:, 0:HALF] - wide[0:HALF], 4.0)
            )
            w_right = table[c, 0:HALF, HALF:Q] * jnp.exp(row[:, HALF:Q] - wide[0:HALF])
            w_corner = table[c, HALF:Q, HALF:Q] * jnp.exp(
                jnp.minimum(row[:, HALF:Q] - wide[HALF:Q], 4.0)
            )
            w_last = jnp.concatenate([w_right.astype(BF16), w_corner.astype(BF16)], axis=0)
            values = values_of(h, c)
            y = jnp.concatenate(
                [
                    jnp.dot(values[:, 0:HALF], w_top.astype(BF16), preferred_element_type=F32),
                    jnp.dot(values, w_last, preferred_element_type=F32),
                ],
                axis=1,
            )
            y = y + skip[h] * values.astype(F32)
            part[c] = y * jnp.concatenate([gate, gate], axis=0)
            scale[c] = erow[c, h:h + 1, :] * gate

        enter[...] = jnp.zeros(enter.shape, F32)
        for d in range(chain - 1, 0, -1):
            @pl.when(rank >= d)
            def _():
                s_copy(h, d, seq - d).wait_recv()
                tail = sgot[d - 1, h, 128:128 + TAIL, :].astype(F32)
                passed = tail[0:1] + tail[1:2]
                same = jnp.where(tail[2:3] == first_id, 1.0, 0.0)
                enter[...] = passed * enter[...] + same * sgot[d - 1, h, 0:128, :].astype(F32)
        state = enter[...]
        for c in range(blocks):
            at = slice(c * Q, (c + 1) * Q)
            carried = jnp.dot(state.astype(BF16), cmt[c], preferred_element_type=F32)
            scaled = scale[c]
            gated = part[c] + carried * jnp.concatenate([scaled, scaled], axis=0)
            gsend[h, at, :] = gated.astype(BF16).T
            if c < blocks - 1:
                state = keep_after(c) * (dec[c, h:h + 1, :] * state + bstate[h, c])
        own_copy(h).start()
        if h < heads - 2:
            for o in order:
                for i in range(pieces):
                    g_copy(h, o, i).start()
    for i in range(pieces):
        for h in range(heads - 2, heads):
            for o in order:
                g_copy(h, o, i).start()

    for h in range(heads):
        own_copy(h).wait()

    pairs = n_head * heads // 2
    width = n_head * heads * 64
    step_rows = 32
    left_lanes = lax.broadcasted_iota(jnp.int32, (step_rows, 128), 1) < 64

    def norm(i, carry):
        at = pl.ds(pl.multiple_of(i * step_rows, step_rows), step_rows)
        square = jnp.zeros((step_rows, 128), F32)
        cross = jnp.zeros((step_rows, 128), F32)
        for j in range(pairs):
            k, m = 2 * j, 2 * j + 1
            one = got[k // heads, k % heads, at, :].astype(F32)
            two = got[m // heads, m % heads, at, :].astype(F32)
            main = jnp.where(left_lanes, one, pltpu.roll(two, 64, 1))
            tan = jnp.where(left_lanes, pltpu.roll(one, 64, 1), two)
            square += main * main
            cross += main * tan
            out_main[at, j * 128:(j + 1) * 128] = main.astype(BF16)
            out_tan[at, j * 128:(j + 1) * 128] = tan.astype(BF16)
        mean_square = jnp.sum(square, axis=1, keepdims=True) / width
        mean_cross = jnp.sum(cross, axis=1, keepdims=True) / width
        inv = lax.rsqrt(mean_square + 1e-05)
        inv_wide = jnp.broadcast_to(inv, (step_rows, 128))
        pull = jnp.broadcast_to(inv * inv * inv * mean_cross, (step_rows, 128))
        for j in range(pairs):
            lanes = slice(j * 128, (j + 1) * 128)
            by = gain[lanes].reshape(1, 128)
            main = out_main[at, lanes].astype(F32)
            tan = out_tan[at, lanes].astype(F32)
            out_main[at, lanes] = (by * main * inv_wide).astype(BF16)
            out_tan[at, lanes] = (by * (tan * inv_wide - main * pull)).astype(BF16)
        return carry

    for i in range(pieces):
        for h in range(heads):
            for o in order:
                g_copy(h, o, i).wait_recv()
        steps = span // step_rows
        lax.fori_loop(i * steps, (i + 1) * steps, norm, 0)

    for h in range(heads):
        for o in order:
            for i in range(pieces):
                g_copy(h, o, i).wait_send()
        for d in range(chain - 1, 0, -1):
            @pl.when(rank + d < chain)
            def _():
                s_copy(h, d, seq + d).wait_send()


def local(n_seq, n_head, xs, dxs, zgate, bmat, cmat, dt_raw, dt_bias, a_rate, d_skip, gain, traj_ids):
    tokens = xs.shape[0]
    heads = dt_raw.shape[0]
    blocks = tokens // Q
    rows = tokens // n_head
    width = xs.shape[1] * n_head
    chain = n_seq // 2
    vmem = pl.BlockSpec(memory_space=pltpu.VMEM)
    hbm = pl.BlockSpec(memory_space=pltpu.HBM)
    span = 128 if rows % 128 == 0 else rows
    return pl.pallas_call(
        functools.partial(kernel, n_seq, n_head, heads, blocks, rows),
        out_shape=[jax.ShapeDtypeStruct((rows, width), BF16)] * 2,
        in_specs=[hbm] * 11,
        out_specs=[vmem] * 2,
        scratch_shapes=[
            pltpu.VMEM((xs.shape[1], tokens), BF16),
            pltpu.VMEM((xs.shape[1], tokens), BF16),
            pltpu.VMEM((xs.shape[1], tokens), BF16),
            pltpu.VMEM(bmat.shape, BF16),
            pltpu.VMEM(cmat.shape, BF16),
            pltpu.VMEM(dt_raw.shape, F32),
            pltpu.SMEM(dt_bias.shape, F32),
            pltpu.SMEM(a_rate.shape, F32),
            pltpu.SMEM(d_skip.shape, F32),
            pltpu.VMEM(gain.shape, F32),
            pltpu.SMEM(traj_ids.shape, jnp.int32),
            pltpu.SemaphoreType.DMA((13,)),
            pltpu.VMEM((8, tokens), F32),
            pltpu.VMEM((heads, blocks, 128, 128), F32),
            pltpu.VMEM((blocks, 8, Q), F32),
            pltpu.VMEM((blocks, 8, Q), F32),
            pltpu.VMEM((blocks, 8, Q), F32),
            pltpu.VMEM((blocks, Q, 8), F32),
            pltpu.VMEM((blocks, 8, 128), F32),
            pltpu.VMEM((blocks, Q, Q), F32),
            pltpu.VMEM((blocks, 128, Q), BF16),
            pltpu.VMEM((blocks, 128, Q), F32),
            pltpu.VMEM((blocks, 64, Q), F32),
            pltpu.VMEM((heads, 128 + TAIL, 128), BF16),
            pltpu.VMEM((chain - 1, heads, 128 + TAIL, 128), BF16),
            pltpu.VMEM((128, 128), F32),
            pltpu.VMEM((heads, tokens, 128), BF16),
            pltpu.VMEM((n_head, heads, rows, 128), BF16),
            pltpu.SemaphoreType.DMA((chain - 1, heads)),
            pltpu.SemaphoreType.DMA((chain - 1, heads)),
            pltpu.SemaphoreType.DMA((n_head - 1, heads, rows // span)),
            pltpu.SemaphoreType.DMA((n_head - 1, heads, rows // span)),
            pltpu.SemaphoreType.DMA((heads,)),
        ],
        compiler_params=pltpu.CompilerParams(
            collective_id=0, has_side_effects=True, vmem_limit_bytes=56 * 2**20
        ),
        name="ssd_layer",
    )(xs.T, dxs.T, zgate.T, bmat, cmat, dt_raw, dt_bias, a_rate, d_skip, gain, traj_ids)


def solution(mesh):
    placed = (
        P("seq", "head"), P("seq", "head"), P("seq", "head"), P("seq", None), P("seq", None),
        P("head", "seq"), P("head"), P("head"), P("head"), P(), P("seq"),
    )
    return jax.shard_map(
        functools.partial(local, mesh.shape["seq"], mesh.shape["head"]),
        mesh=mesh,
        in_specs=placed,
        out_specs=(P(("seq", "head"), None), P(("seq", "head"), None)),
        check_vma=False,
    )
```

```python
import functools

import jax
import jax.numpy as jnp
from jax import lax
from jax.experimental import pallas as pl
from jax.experimental.pallas import tpu as pltpu
from jax.sharding import PartitionSpec as P

Q = 256
HALF = 128
TAIL = 16
MESH = pl.DeviceIdType.MESH
F32 = jnp.float32
BF16 = jnp.bfloat16


def column_of(ref, count):
    place = lax.broadcasted_iota(jnp.int32, (8, 1), 0)
    column = jnp.zeros((8, 1), F32)
    for h in range(count):
        column = jnp.where(place == h, ref[h], column)
    return column


def by_rows(one, two):
    return lax.dot_general(one, two, (((1,), (1,)), ((), ())), preferred_element_type=F32)


def kernel(
    n_seq, n_head, heads, blocks, rows,
    xs_hbm, dxs_hbm, zg_hbm, bm_hbm, cm_hbm, dt_hbm, bias_hbm, rate_hbm, skip_hbm, traj_hbm,
    got,
    xs, dxs, zg, bm, cm, dt, bias, rate, skip, traj, in_sem,
    dt8, bstate, lrow, wrow, erow, lcol, dec, table, cmt, part, scale, smsg, sgot, enter, gsend,
    s_send, s_recv, g_send, g_recv, own_sem,
):
    chain = n_seq // 2
    seq = lax.axis_index("seq")
    me = lax.axis_index("head")
    rank = lax.rem(seq, chain)
    base = seq - rank

    fetches = [
        pltpu.make_async_copy(source, target, in_sem.at[i])
        for i, (source, target) in enumerate((
            (dt_hbm, dt), (bias_hbm, bias), (rate_hbm, rate),
            (xs_hbm.at[0:64], xs.at[0:64]), (dxs_hbm.at[0:64], dxs.at[0:64]),
            (bm_hbm, bm), (traj_hbm, traj),
            (xs_hbm.at[64:], xs.at[64:]), (dxs_hbm.at[64:], dxs.at[64:]),
            (cm_hbm, cm), (zg_hbm, zg), (skip_hbm, skip),
        ))
    ]
    for fetch in fetches:
        fetch.start()

    barrier = pltpu.get_barrier_semaphore()
    for o in range(1, n_head):
        pl.semaphore_signal(
            barrier, inc=1, device_id=(seq, lax.rem(me + o, n_head)), device_id_type=MESH
        )
    for o in range(1, chain):
        pl.semaphore_signal(
            barrier, inc=1, device_id=(base + lax.rem(rank + o, chain), me), device_id_type=MESH
        )

    dt8[...] = jnp.zeros(dt8.shape, F32)
    for fetch in fetches[0:3]:
        fetch.wait()
    dt8[0:heads, :] = dt[...]
    step_all = jax.nn.softplus(dt8[...] + column_of(bias, heads))
    fall_all = step_all * column_of(rate, heads)
    step = jnp.concatenate([step_all[:, c * Q:(c + 1) * Q] for c in range(blocks)], axis=0)
    fall = jnp.concatenate([fall_all[:, c * Q:(c + 1) * Q] for c in range(blocks)], axis=0)
    first = fall.astype(BF16)
    rest = fall - first.astype(F32)
    second = rest.astype(BF16)
    third = (rest - second.astype(F32)).astype(BF16)
    upper = (
        lax.broadcasted_iota(jnp.int32, (Q, Q), 0) <= lax.broadcasted_iota(jnp.int32, (Q, Q), 1)
    ).astype(F32).astype(BF16)
    sums = [jnp.dot(x, upper, preferred_element_type=F32) for x in (first, second, third)]
    log_decay = -(sums[0] + (sums[1] + sums[2]))
    end_log = log_decay[:, Q - 1:Q]
    weight_in = step * jnp.exp(end_log - log_decay)
    end_wide = jnp.broadcast_to(end_log, (blocks * 8, 128))
    end_decay = jnp.exp(end_wide)
    whole_log = end_wide[0:8]
    for c in range(1, blocks):
        whole_log = whole_log + end_wide[c * 8:(c + 1) * 8]
    factor = jnp.exp(whole_log)
    for c in range(blocks):
        wrow[c] = weight_in[c * 8:(c + 1) * 8]
        dec[c] = end_decay[c * 8:(c + 1) * 8]

    def keep_after(c):
        return jnp.where(traj[c] == traj[c + 1], 1.0, 0.0).astype(F32)

    def values_of(h, c):
        low, at = h * 64, slice(c * Q, (c + 1) * Q)
        return jnp.concatenate([xs[low:low + 64, at], dxs[low:low + 64, at]], axis=0)

    def s_copy(h, d, to):
        return pltpu.make_async_remote_copy(
            src_ref=smsg.at[h],
            dst_ref=sgot.at[d - 1, h],
            send_sem=s_send.at[d - 1, h],
            recv_sem=s_recv.at[d - 1, h],
            device_id=(to, me),
            device_id_type=MESH,
        )

    for fetch in fetches[3:7]:
        fetch.wait()
    last_id = traj[blocks - 1].astype(F32)
    tail_row = lax.broadcasted_iota(jnp.int32, (TAIL, 128), 0)
    for h in range(heads):
        if h == 1:
            for fetch in fetches[7:9]:
                fetch.wait()
        state = None
        for c in range(blocks):
            weighted = (values_of(h, c).astype(F32) * wrow[c, h:h + 1, :]).astype(BF16)
            block = jnp.dot(weighted, bm[c * Q:(c + 1) * Q, :], preferred_element_type=F32)
            bstate[h, c] = block
            if c == 0:
                state = block
            else:
                state = keep_after(c - 1) * (dec[c, h:h + 1, :] * state) + block
        smsg[h, 0:128, :] = state.astype(BF16)
        whole = jnp.broadcast_to(factor[h:h + 1, :], (TAIL, 128))
        high = whole.astype(BF16).astype(F32)
        tail = jnp.where(tail_row == 0, high, jnp.where(tail_row == 1, whole - high, last_id))
        smsg[h, 128:128 + TAIL, :] = tail.astype(BF16)
        if h == 0:
            pl.semaphore_wait(barrier, (n_head - 1) + (chain - 1))
        for d in range(chain - 1, 0, -1):
            @pl.when(rank + d < chain)
            def _():
                s_copy(h, d, seq + d).start()

    for fetch in fetches[9:]:
        fetch.wait()
    log_row = log_decay - jnp.log(step)
    decay = jnp.exp(log_decay)
    turned = jnp.concatenate([log_row, jnp.zeros((128 - blocks * 8, Q), F32)], axis=0).T
    row_at = lax.broadcasted_iota(jnp.int32, (Q, Q), 0)
    col_at = lax.broadcasted_iota(jnp.int32, (Q, Q), 1)
    causal = row_at <= col_at
    for c in range(blocks):
        lrow[c] = log_decay[c * 8:(c + 1) * 8]
        erow[c] = decay[c * 8:(c + 1) * 8]
        lcol[c] = turned[:, c * 8:(c + 1) * 8]
        at = slice(c * Q, (c + 1) * Q)
        table[c] = jnp.where(causal, by_rows(bm[at, :], cm[at, :]), 0.0)
        cmt[c] = cm[at, :].astype(F32).T.astype(BF16)

    def g_copy(h, o):
        to = lax.rem(me + o, n_head)
        return pltpu.make_async_remote_copy(
            src_ref=gsend.at[h, pl.ds(pl.multiple_of(to * rows, 16), rows), :],
            dst_ref=got.at[me, h],
            send_sem=g_send.at[o - 1, h],
            recv_sem=g_recv.at[o - 1, h],
            device_id=(seq, to),
            device_id_type=MESH,
        )

    def own_copy(h):
        return pltpu.make_async_copy(
            gsend.at[h, pl.ds(pl.multiple_of(me * rows, 16), rows), :], got.at[me, h], own_sem.at[h]
        )

    order = sorted(range(1, n_head), key=lambda o: abs(o - n_head // 2))
    first_id = traj[0].astype(F32)
    for h in range(heads):
        low = h * 64
        for c in range(blocks):
            at = slice(c * Q, (c + 1) * Q)
            row = lrow[c, h:h + 1, :]
            wide = jnp.broadcast_to(lcol[c, :, h:h + 1], (Q, HALF))
            gate_in = zg[low:low + 64, at].astype(F32)
            gate = gate_in / (1.0 + jnp.exp(-gate_in))
            w_top = table[c, 0:HALF, 0:HALF] * jnp.exp(
                jnp.minimum(row[:, 0:HALF] - wide[0:HALF], 4.0)
            )
            w_right = table[c, 0:HALF, HALF:Q] * jnp.exp(row[:, HALF:Q] - wide[0:HALF])
            w_corner = table[c, HALF:Q, HALF:Q] * jnp.exp(
                jnp.minimum(row[:, HALF:Q] - wide[HALF:Q], 4.0)
            )
            w_last = jnp.concatenate([w_right.astype(BF16), w_corner.astype(BF16)], axis=0)
            values = values_of(h, c)
            y = jnp.concatenate(
                [
                    jnp.dot(values[:, 0:HALF], w_top.astype(BF16), preferred_element_type=F32),
                    jnp.dot(values, w_last, preferred_element_type=F32),
                ],
                axis=1,
            )
            y = y + skip[h] * values.astype(F32)
            part[c] = y * jnp.concatenate([gate, gate], axis=0)
            scale[c] = erow[c, h:h + 1, :] * gate

        enter[...] = jnp.zeros(enter.shape, F32)
        for d in range(chain - 1, 0, -1):
            @pl.when(rank >= d)
            def _():
                s_copy(h, d, seq - d).wait_recv()
                tail = sgot[d - 1, h, 128:128 + TAIL, :].astype(F32)
                passed = tail[0:1] + tail[1:2]
                same = jnp.where(tail[2:3] == first_id, 1.0, 0.0)
                enter[...] = passed * enter[...] + same * sgot[d - 1, h, 0:128, :].astype(F32)
        state = enter[...]
        for c in range(blocks):
            at = slice(c * Q, (c + 1) * Q)
            carried = jnp.dot(state.astype(BF16), cmt[c], preferred_element_type=F32)
            scaled = scale[c]
            gated = part[c] + carried * jnp.concatenate([scaled, scaled], axis=0)
            gsend[h, at, :] = gated.astype(BF16).T
            if c < blocks - 1:
                state = keep_after(c) * (dec[c, h:h + 1, :] * state + bstate[h, c])
        own_copy(h).start()
        for o in order:
            g_copy(h, o).start()

    for h in range(heads):
        own_copy(h).wait()
        for o in order:
            g_copy(h, o).wait()
        for d in range(chain - 1, 0, -1):
            @pl.when(rank + d < chain)
            def _():
                s_copy(h, d, seq + d).wait_send()


def norm_kernel(heads, got, gain, out_main, out_tan):
    n_head, _, rows, _ = got.shape
    pairs = n_head * heads // 2
    width = n_head * heads * 64
    span = 32
    left_lanes = lax.broadcasted_iota(jnp.int32, (span, 128), 1) < 64
    for i in range(rows // span):
        at = slice(i * span, (i + 1) * span)
        square = jnp.zeros((span, 128), F32)
        cross = jnp.zeros((span, 128), F32)
        for j in range(pairs):
            k, m = 2 * j, 2 * j + 1
            one = got[k // heads, k % heads, at, :].astype(F32)
            two = got[m // heads, m % heads, at, :].astype(F32)
            main = jnp.where(left_lanes, one, pltpu.roll(two, 64, 1))
            tan = jnp.where(left_lanes, pltpu.roll(one, 64, 1), two)
            square += main * main
            cross += main * tan
            out_main[at, j * 128:(j + 1) * 128] = main.astype(BF16)
            out_tan[at, j * 128:(j + 1) * 128] = tan.astype(BF16)
        mean_square = jnp.sum(square, axis=1, keepdims=True) / width
        mean_cross = jnp.sum(cross, axis=1, keepdims=True) / width
        inv = lax.rsqrt(mean_square + 1e-05)
        inv_wide = jnp.broadcast_to(inv, (span, 128))
        pull = jnp.broadcast_to(inv * inv * inv * mean_cross, (span, 128))
        for j in range(pairs):
            lanes = slice(j * 128, (j + 1) * 128)
            by = gain[lanes].reshape(1, 128)
            main = out_main[at, lanes].astype(F32)
            tan = out_tan[at, lanes].astype(F32)
            out_main[at, lanes] = (by * main * inv_wide).astype(BF16)
            out_tan[at, lanes] = (by * (tan * inv_wide - main * pull)).astype(BF16)


def local(n_seq, n_head, xs, dxs, zgate, bmat, cmat, dt_raw, dt_bias, a_rate, d_skip, gain, traj_ids):
    tokens = xs.shape[0]
    heads = dt_raw.shape[0]
    blocks = tokens // Q
    rows = tokens // n_head
    width = xs.shape[1] * n_head
    chain = n_seq // 2
    hbm = pl.BlockSpec(memory_space=pltpu.HBM)
    got = pl.pallas_call(
        functools.partial(kernel, n_seq, n_head, heads, blocks, rows),
        out_shape=jax.ShapeDtypeStruct((n_head, heads, rows, 128), BF16),
        in_specs=[hbm] * 10,
        out_specs=hbm,
        scratch_shapes=[
            pltpu.VMEM((xs.shape[1], tokens), BF16),
            pltpu.VMEM((xs.shape[1], tokens), BF16),
            pltpu.VMEM((xs.shape[1], tokens), BF16),
            pltpu.VMEM(bmat.shape, BF16),
            pltpu.VMEM(cmat.shape, BF16),
            pltpu.VMEM(dt_raw.shape, F32),
            pltpu.SMEM(dt_bias.shape, F32),
            pltpu.SMEM(a_rate.shape, F32),
            pltpu.SMEM(d_skip.shape, F32),
            pltpu.SMEM(traj_ids.shape, jnp.int32),
            pltpu.SemaphoreType.DMA((12,)),
            pltpu.VMEM((8, tokens), F32),
            pltpu.VMEM((heads, blocks, 128, 128), F32),
            pltpu.VMEM((blocks, 8, Q), F32),
            pltpu.VMEM((blocks, 8, Q), F32),
            pltpu.VMEM((blocks, 8, Q), F32),
            pltpu.VMEM((blocks, Q, 8), F32),
            pltpu.VMEM((blocks, 8, 128), F32),
            pltpu.VMEM((blocks, Q, Q), F32),
            pltpu.VMEM((blocks, 128, Q), BF16),
            pltpu.VMEM((blocks, 128, Q), F32),
            pltpu.VMEM((blocks, 64, Q), F32),
            pltpu.VMEM((heads, 128 + TAIL, 128), BF16),
            pltpu.VMEM((chain - 1, heads, 128 + TAIL, 128), BF16),
            pltpu.VMEM((128, 128), F32),
            pltpu.VMEM((heads, tokens, 128), BF16),
            pltpu.SemaphoreType.DMA((chain - 1, heads)),
            pltpu.SemaphoreType.DMA((chain - 1, heads)),
            pltpu.SemaphoreType.DMA((n_head - 1, heads)),
            pltpu.SemaphoreType.DMA((n_head - 1, heads)),
            pltpu.SemaphoreType.DMA((heads,)),
        ],
        compiler_params=pltpu.CompilerParams(
            collective_id=0, has_side_effects=True, vmem_limit_bytes=56 * 2**20
        ),
        name="ssd_layer",
    )(xs.T, dxs.T, zgate.T, bmat, cmat, dt_raw, dt_bias, a_rate, d_skip, traj_ids)
    part_rows = 96
    return pl.pallas_call(
        functools.partial(norm_kernel, heads),
        grid=(rows // part_rows,),
        out_shape=[jax.ShapeDtypeStruct((rows, width), BF16)] * 2,
        in_specs=[
            pl.BlockSpec((n_head, heads, part_rows, 128), lambda i: (0, 0, i, 0)),
            pl.BlockSpec(gain.shape, lambda i: (0,)),
        ],
        out_specs=[pl.BlockSpec((part_rows, width), lambda i: (i, 0))] * 2,
        compiler_params=pltpu.CompilerParams(vmem_limit_bytes=56 * 2**20),
        name="norm",
    )(got, gain)


def solution(mesh):
    placed = (
        P("seq", "head"), P("seq", "head"), P("seq", "head"), P("seq", None), P("seq", None),
        P("head", "seq"), P("head"), P("head"), P("head"), P(), P("seq"),
    )
    return jax.shard_map(
        functools.partial(local, mesh.shape["seq"], mesh.shape["head"]),
        mesh=mesh,
        in_specs=placed,
        out_specs=(P(("seq", "head"), None), P(("seq", "head"), None)),
        check_vma=False,
    )
```

```python
import functools

import jax
import jax.numpy as jnp
from jax import lax
from jax.experimental import pallas as pl
from jax.experimental.pallas import tpu as pltpu
from jax.sharding import PartitionSpec as P

Q = 256
HALF = 128
TAIL = 16
MESH = pl.DeviceIdType.MESH
F32 = jnp.float32
BF16 = jnp.bfloat16


def column_of(ref, count):
    place = lax.broadcasted_iota(jnp.int32, (8, 1), 0)
    column = jnp.zeros((8, 1), F32)
    for h in range(count):
        column = jnp.where(place == h, ref[h], column)
    return column


def by_rows(one, two):
    return lax.dot_general(one, two, (((1,), (1,)), ((), ())), preferred_element_type=F32)


def kernel(
    n_seq, n_head, heads, blocks, rows,
    xs_hbm, dxs_hbm, zg_hbm, bm_hbm, cm_hbm, dt_hbm, bias_hbm, rate_hbm, skip_hbm, traj_hbm,
    got,
    xs, dxs, zg, bm, cm, dt, bias, rate, skip, traj, in_sem,
    dt8, bstate, lrow, wrow, erow, lcol, dec, table, cmt, part, scale, smsg, sgot, enter, gsend,
    s_send, s_recv, g_send, g_recv, own_sem,
):
    chain = n_seq // 2
    seq = lax.axis_index("seq")
    me = lax.axis_index("head")
    rank = lax.rem(seq, chain)
    base = seq - rank

    fetches = [
        pltpu.make_async_copy(source, target, in_sem.at[i])
        for i, (source, target) in enumerate((
            (dt_hbm, dt), (bias_hbm, bias), (rate_hbm, rate),
            (xs_hbm.at[0:64], xs.at[0:64]), (dxs_hbm.at[0:64], dxs.at[0:64]),
            (bm_hbm, bm), (traj_hbm, traj),
            (xs_hbm.at[64:], xs.at[64:]), (dxs_hbm.at[64:], dxs.at[64:]),
            (cm_hbm, cm), (zg_hbm, zg), (skip_hbm, skip),
        ))
    ]
    for fetch in fetches:
        fetch.start()

    barrier = pltpu.get_barrier_semaphore()
    for o in range(1, n_head):
        pl.semaphore_signal(
            barrier, inc=1, device_id=(seq, lax.rem(me + o, n_head)), device_id_type=MESH
        )
    for o in range(1, chain):
        pl.semaphore_signal(
            barrier, inc=1, device_id=(base + lax.rem(rank + o, chain), me), device_id_type=MESH
        )

    dt8[...] = jnp.zeros(dt8.shape, F32)
    for fetch in fetches[0:3]:
        fetch.wait()
    dt8[0:heads, :] = dt[...]
    step_all = jax.nn.softplus(dt8[...] + column_of(bias, heads))
    fall_all = step_all * column_of(rate, heads)
    step = jnp.concatenate([step_all[:, c * Q:(c + 1) * Q] for c in range(blocks)], axis=0)
    fall = jnp.concatenate([fall_all[:, c * Q:(c + 1) * Q] for c in range(blocks)], axis=0)
    first = fall.astype(BF16)
    rest = fall - first.astype(F32)
    second = rest.astype(BF16)
    third = (rest - second.astype(F32)).astype(BF16)
    upper = (
        lax.broadcasted_iota(jnp.int32, (Q, Q), 0) <= lax.broadcasted_iota(jnp.int32, (Q, Q), 1)
    ).astype(F32).astype(BF16)
    sums = [jnp.dot(x, upper, preferred_element_type=F32) for x in (first, second, third)]
    log_decay = -(sums[0] + (sums[1] + sums[2]))
    end_log = log_decay[:, Q - 1:Q]
    weight_in = step * jnp.exp(end_log - log_decay)
    end_wide = jnp.broadcast_to(end_log, (blocks * 8, 128))
    end_decay = jnp.exp(end_wide)
    whole_log = end_wide[0:8]
    for c in range(1, blocks):
        whole_log = whole_log + end_wide[c * 8:(c + 1) * 8]
    factor = jnp.exp(whole_log)
    for c in range(blocks):
        wrow[c] = weight_in[c * 8:(c + 1) * 8]
        dec[c] = end_decay[c * 8:(c + 1) * 8]

    def keep_after(c):
        return jnp.where(traj[c] == traj[c + 1], 1.0, 0.0).astype(F32)

    def values_of(h, c):
        low, at = h * 64, slice(c * Q, (c + 1) * Q)
        return jnp.concatenate([xs[low:low + 64, at], dxs[low:low + 64, at]], axis=0)

    def s_copy(h, d, to):
        return pltpu.make_async_remote_copy(
            src_ref=smsg.at[h],
            dst_ref=sgot.at[d - 1, h],
            send_sem=s_send.at[d - 1, h],
            recv_sem=s_recv.at[d - 1, h],
            device_id=(to, me),
            device_id_type=MESH,
        )

    for fetch in fetches[3:7]:
        fetch.wait()
    last_id = traj[blocks - 1].astype(F32)
    tail_row = lax.broadcasted_iota(jnp.int32, (TAIL, 128), 0)
    for h in range(heads):
        if h == 1:
            for fetch in fetches[7:9]:
                fetch.wait()
        state = None
        for c in range(blocks):
            weighted = (values_of(h, c).astype(F32) * wrow[c, h:h + 1, :]).astype(BF16)
            block = jnp.dot(weighted, bm[c * Q:(c + 1) * Q, :], preferred_element_type=F32)
            bstate[h, c] = block
            if c == 0:
                state = block
            else:
                state = keep_after(c - 1) * (dec[c, h:h + 1, :] * state) + block
        smsg[h, 0:128, :] = state.astype(BF16)
        whole = jnp.broadcast_to(factor[h:h + 1, :], (TAIL, 128))
        high = whole.astype(BF16).astype(F32)
        tail = jnp.where(tail_row == 0, high, jnp.where(tail_row == 1, whole - high, last_id))
        smsg[h, 128:128 + TAIL, :] = tail.astype(BF16)
        if h == 0:
            pl.semaphore_wait(barrier, (n_head - 1) + (chain - 1))
        for d in range(chain - 1, 0, -1):
            @pl.when(rank + d < chain)
            def _():
                s_copy(h, d, seq + d).start()

    for fetch in fetches[9:]:
        fetch.wait()
    log_row = log_decay - jnp.log(step)
    decay = jnp.exp(log_decay)
    turned = jnp.concatenate([log_row, jnp.zeros((128 - blocks * 8, Q), F32)], axis=0).T
    row_at = lax.broadcasted_iota(jnp.int32, (Q, Q), 0)
    col_at = lax.broadcasted_iota(jnp.int32, (Q, Q), 1)
    causal = row_at <= col_at
    for c in range(blocks):
        lrow[c] = log_decay[c * 8:(c + 1) * 8]
        erow[c] = decay[c * 8:(c + 1) * 8]
        lcol[c] = turned[:, c * 8:(c + 1) * 8]
        at = slice(c * Q, (c + 1) * Q)
        table[c] = jnp.where(causal, by_rows(bm[at, :], cm[at, :]), 0.0)
        cmt[c] = cm[at, :].astype(F32).T.astype(BF16)

    def g_copy(h, o):
        to = lax.rem(me + o, n_head)
        return pltpu.make_async_remote_copy(
            src_ref=gsend.at[h, pl.ds(pl.multiple_of(to * rows, 16), rows), :],
            dst_ref=got.at[me, h],
            send_sem=g_send.at[o - 1, h],
            recv_sem=g_recv.at[o - 1, h],
            device_id=(seq, to),
            device_id_type=MESH,
        )

    def own_copy(h):
        return pltpu.make_async_copy(
            gsend.at[h, pl.ds(pl.multiple_of(me * rows, 16), rows), :], got.at[me, h], own_sem.at[h]
        )

    order = sorted(range(1, n_head), key=lambda o: abs(o - n_head // 2))
    first_id = traj[0].astype(F32)
    for h in range(heads):
        low = h * 64
        for c in range(blocks):
            at = slice(c * Q, (c + 1) * Q)
            row = lrow[c, h:h + 1, :]
            wide = jnp.broadcast_to(lcol[c, :, h:h + 1], (Q, HALF))
            gate_in = zg[low:low + 64, at].astype(F32)
            gate = gate_in / (1.0 + jnp.exp(-gate_in))
            w_top = table[c, 0:HALF, 0:HALF] * jnp.exp(
                jnp.minimum(row[:, 0:HALF] - wide[0:HALF], 4.0)
            )
            w_right = table[c, 0:HALF, HALF:Q] * jnp.exp(row[:, HALF:Q] - wide[0:HALF])
            w_corner = table[c, HALF:Q, HALF:Q] * jnp.exp(
                jnp.minimum(row[:, HALF:Q] - wide[HALF:Q], 4.0)
            )
            w_last = jnp.concatenate([w_right.astype(BF16), w_corner.astype(BF16)], axis=0)
            values = values_of(h, c)
            y = jnp.concatenate(
                [
                    jnp.dot(values[:, 0:HALF], w_top.astype(BF16), preferred_element_type=F32),
                    jnp.dot(values, w_last, preferred_element_type=F32),
                ],
                axis=1,
            )
            y = y + skip[h] * values.astype(F32)
            part[c] = y * jnp.concatenate([gate, gate], axis=0)
            scale[c] = erow[c, h:h + 1, :] * gate

        enter[...] = jnp.zeros(enter.shape, F32)
        for d in range(chain - 1, 0, -1):
            @pl.when(rank >= d)
            def _():
                s_copy(h, d, seq - d).wait_recv()
                tail = sgot[d - 1, h, 128:128 + TAIL, :].astype(F32)
                passed = tail[0:1] + tail[1:2]
                same = jnp.where(tail[2:3] == first_id, 1.0, 0.0)
                enter[...] = passed * enter[...] + same * sgot[d - 1, h, 0:128, :].astype(F32)
        state = enter[...]
        for c in range(blocks):
            at = slice(c * Q, (c + 1) * Q)
            carried = jnp.dot(state.astype(BF16), cmt[c], preferred_element_type=F32)
            scaled = scale[c]
            gated = part[c] + carried * jnp.concatenate([scaled, scaled], axis=0)
            gsend[h, at, :] = gated.astype(BF16).T
            if c < blocks - 1:
                state = keep_after(c) * (dec[c, h:h + 1, :] * state + bstate[h, c])
        own_copy(h).start()
        for o in order:
            g_copy(h, o).start()

    for h in range(heads):
        own_copy(h).wait()
        for o in order:
            g_copy(h, o).wait()
        for d in range(chain - 1, 0, -1):
            @pl.when(rank + d < chain)
            def _():
                s_copy(h, d, seq + d).wait_send()


def norm_kernel(heads, got, gain, out_main, out_tan):
    n_head, _, rows, _ = got.shape
    pairs = n_head * heads // 2
    width = n_head * heads * 64
    span = 32
    for i in range(rows // span):
        at = slice(i * span, (i + 1) * span)
        square = jnp.zeros((span, 128), F32)
        cross = jnp.zeros((span, 128), F32)
        for j in range(pairs):
            k, m = 2 * j, 2 * j + 1
            one = got[k // heads, k % heads, at, :]
            two = got[m // heads, m % heads, at, :]
            main = jnp.concatenate([one[:, 0:64], two[:, 0:64]], axis=1)
            tan = jnp.concatenate([one[:, 64:128], two[:, 64:128]], axis=1)
            out_main[at, j * 128:(j + 1) * 128] = main
            out_tan[at, j * 128:(j + 1) * 128] = tan
            wide = main.astype(F32)
            square += wide * wide
            cross += wide * tan.astype(F32)
        mean_square = jnp.sum(square, axis=1, keepdims=True) / width
        mean_cross = jnp.sum(cross, axis=1, keepdims=True) / width
        inv = lax.rsqrt(mean_square + 1e-05)
        inv_wide = jnp.broadcast_to(inv, (span, 128))
        pull = jnp.broadcast_to(inv * inv * inv * mean_cross, (span, 128))
        for j in range(pairs):
            lanes = slice(j * 128, (j + 1) * 128)
            by = gain[lanes].reshape(1, 128)
            main = out_main[at, lanes].astype(F32)
            tan = out_tan[at, lanes].astype(F32)
            out_main[at, lanes] = (by * main * inv_wide).astype(BF16)
            out_tan[at, lanes] = (by * (tan * inv_wide - main * pull)).astype(BF16)


def local(n_seq, n_head, xs, dxs, zgate, bmat, cmat, dt_raw, dt_bias, a_rate, d_skip, gain, traj_ids):
    tokens = xs.shape[0]
    heads = dt_raw.shape[0]
    blocks = tokens // Q
    rows = tokens // n_head
    width = xs.shape[1] * n_head
    chain = n_seq // 2
    hbm = pl.BlockSpec(memory_space=pltpu.HBM)
    got = pl.pallas_call(
        functools.partial(kernel, n_seq, n_head, heads, blocks, rows),
        out_shape=jax.ShapeDtypeStruct((n_head, heads, rows, 128), BF16),
        in_specs=[hbm] * 10,
        out_specs=hbm,
        scratch_shapes=[
            pltpu.VMEM((xs.shape[1], tokens), BF16),
            pltpu.VMEM((xs.shape[1], tokens), BF16),
            pltpu.VMEM((xs.shape[1], tokens), BF16),
            pltpu.VMEM(bmat.shape, BF16),
            pltpu.VMEM(cmat.shape, BF16),
            pltpu.VMEM(dt_raw.shape, F32),
            pltpu.SMEM(dt_bias.shape, F32),
            pltpu.SMEM(a_rate.shape, F32),
            pltpu.SMEM(d_skip.shape, F32),
            pltpu.SMEM(traj_ids.shape, jnp.int32),
            pltpu.SemaphoreType.DMA((12,)),
            pltpu.VMEM((8, tokens), F32),
            pltpu.VMEM((heads, blocks, 128, 128), F32),
            pltpu.VMEM((blocks, 8, Q), F32),
            pltpu.VMEM((blocks, 8, Q), F32),
            pltpu.VMEM((blocks, 8, Q), F32),
            pltpu.VMEM((blocks, Q, 8), F32),
            pltpu.VMEM((blocks, 8, 128), F32),
            pltpu.VMEM((blocks, Q, Q), F32),
            pltpu.VMEM((blocks, 128, Q), BF16),
            pltpu.VMEM((blocks, 128, Q), F32),
            pltpu.VMEM((blocks, 64, Q), F32),
            pltpu.VMEM((heads, 128 + TAIL, 128), BF16),
            pltpu.VMEM((chain - 1, heads, 128 + TAIL, 128), BF16),
            pltpu.VMEM((128, 128), F32),
            pltpu.VMEM((heads, tokens, 128), BF16),
            pltpu.SemaphoreType.DMA((chain - 1, heads)),
            pltpu.SemaphoreType.DMA((chain - 1, heads)),
            pltpu.SemaphoreType.DMA((n_head - 1, heads)),
            pltpu.SemaphoreType.DMA((n_head - 1, heads)),
            pltpu.SemaphoreType.DMA((heads,)),
        ],
        compiler_params=pltpu.CompilerParams(
            collective_id=0, has_side_effects=True, vmem_limit_bytes=56 * 2**20
        ),
        name="ssd_layer",
    )(xs.T, dxs.T, zgate.T, bmat, cmat, dt_raw, dt_bias, a_rate, d_skip, traj_ids)
    part_rows = 96
    return pl.pallas_call(
        functools.partial(norm_kernel, heads),
        grid=(rows // part_rows,),
        out_shape=[jax.ShapeDtypeStruct((rows, width), BF16)] * 2,
        in_specs=[
            pl.BlockSpec((n_head, heads, part_rows, 128), lambda i: (0, 0, i, 0)),
            pl.BlockSpec(gain.shape, lambda i: (0,)),
        ],
        out_specs=[pl.BlockSpec((part_rows, width), lambda i: (i, 0))] * 2,
        compiler_params=pltpu.CompilerParams(vmem_limit_bytes=56 * 2**20),
        name="norm",
    )(got, gain)


def solution(mesh):
    placed = (
        P("seq", "head"), P("seq", "head"), P("seq", "head"), P("seq", None), P("seq", None),
        P("head", "seq"), P("head"), P("head"), P("head"), P(), P("seq"),
    )
    return jax.shard_map(
        functools.partial(local, mesh.shape["seq"], mesh.shape["head"]),
        mesh=mesh,
        in_specs=placed,
        out_specs=(P(("seq", "head"), None), P(("seq", "head"), None)),
        check_vma=False,
    )
```
